128 devices in a mesh: grp: 32 (over z, x, core), tp: 4 (over y).
Axes of the slice: x: 4, y: 4, z: 4, core: 2. Of those that a mesh axis runs over, the one named last changes fastest.
Arguments:
- hidden_in: bfloat16 [1024, 2048], P('grp'), may hold values from -3 to 3
- attn_gain: float32 [2048], replicated, may hold values from 0.5 to 2
- ffn_gain: float32 [2048], replicated, may hold values from 0.5 to 2
- w_query: bfloat16 [2048, 4096], P(None, 'tp'), may hold values from -0.125 to 0.125
- w_key: bfloat16 [2048, 512], P(None, 'tp'), may hold values from -0.125 to 0.125
- w_value: bfloat16 [2048, 512], P(None, 'tp'), may hold values from -0.125 to 0.125
- q_gain: float32 [128], replicated, as said below
- k_gain: float32 [128], replicated, may hold values from 0.5 to 2
- key_cache: bfloat16 [1024, 4, 512, 128], P('grp', 'tp'), may hold values from -32 to 32
- value_cache: bfloat16 [1024, 4, 512, 128], P('grp', 'tp'), may hold values from -6 to 6
- w_out: bfloat16 [4096, 2048], P('tp'), may hold values from -0.09375 to 0.09375
- w_router: bfloat16 [2048, 128], replicated, may hold values from -0.03125 to 0.03125
- w_gate: bfloat16 [128, 2048, 768], P('grp', None, 'tp'), may hold values from -0.125 to 0.125
- w_up: bfloat16 [128, 2048, 768], P('grp', None, 'tp'), may hold values from -0.125 to 0.125
- w_down: bfloat16 [128, 768, 2048], P('grp', 'tp'), may hold values from -0.21875 to 0.21875
- cache_len: int32 [1024], P('grp'), may hold values from 1 to 512, as said below
- expert_ids: int32 [1024, 8], P('grp'), may hold values from 0 to 127, all different within a row; in each aligned block of 32 rows (0 to 31, 32 to 63, ...) at most 4 rows name the same one
Outputs:
- mixed: bfloat16 [1024, 2048], P('grp', 'tp')
The draws below stay inside these ranges and needn't reach their ends.
Inputs may be any that keep to these rules, and one draw needn't show every extreme that they name: `expert_ids`: each row names 8 different experts. Among the 32 rows of one index of grp (aligned blocks) no expert is named by more than 4 rows, a bound that some block reaches. `cache_len`: some request has exactly 512 cached tokens. `q_gain`: positive gains.
All inputs are finite; a program needn't handle non-finite values.
Results may differ from the reference program's by a relative error of at most 0.02.
Values may be sent and summed in bfloat16 or wider, within the bound.
A program may use at most 128 MiB of HBM per device.

```python
import math
import jax
import jax.numpy as jnp
import numpy as np
from jax import lax

D = 2048
QH = 32
KVH = 4
HD = 128
FF = 768
TOPK = 8
REQ = 32
LMAX = 512
EXPERTS = 128
REQ_TOTAL = 1024
CAP = 4
N_GRP = 32


def draw_q_gain(key, part):
    key = jax.random.fold_in(key, 11)
    return jnp.exp(jax.random.uniform(key, (HD,), jnp.float32, math.log(0.5), math.log(2.0)))


def draw_key_cache(key, part):
    key = jax.random.fold_in(key, 13)
    base_key = jax.random.fold_in(key, 0)
    shape = (REQ_TOTAL, KVH, LMAX, HD)
    return jnp.clip(jax.random.normal(base_key, shape, jnp.float32), -6.0, 6.0).astype(jnp.bfloat16)


def draw_cache_len(key, part):
    key = jax.random.fold_in(key, 7)
    first, second, third = jax.random.split(key, 3)
    groups = REQ_TOTAL // REQ
    ceiling = jax.random.randint(first, (groups, 1), LMAX // 4, LMAX + 1)
    raw = jax.random.randint(second, (groups, REQ), 0, 2 ** 20)
    lengths = (1 + raw * ceiling // 2 ** 20).reshape(-1)
    chosen = jax.random.randint(third, (), 0, REQ_TOTAL)
    positions = jnp.arange(REQ_TOTAL, dtype=jnp.int32)
    return jnp.where(positions == chosen, LMAX, jnp.minimum(lengths, LMAX)).astype(jnp.int32)


def steps_of(stream_key, extent, shards, least, top_value):
    def one(dim, parts):
        steps = jax.random.uniform(jax.random.fold_in(jax.random.fold_in(stream_key, 6), dim), (parts,), jnp.float32, least / len(shards), top_value / len(shards))
        return jnp.repeat(jnp.exp(steps), extent[dim] // parts).reshape((-1,) + (1,) * (len(extent) - dim - 1))

    loudness = one(*shards[0])
    for cut in shards[1:]:
        loudness = loudness * one(*cut)
    return loudness


def assign_block(own_key, own, number, rows, count, top, reach, skew):
    order = jax.random.permutation(own_key, count)
    crowded, usual = load_shares(count, rows * top, reach, skew, True), load_shares(count, rows * top, reach, skew, False)
    places = jnp.arange(count)

    def named(sizes, offset_by):
        used = int((sizes > 0).sum())
        fixed = max(1, used // 4)
        moved = fixed + (places - fixed + offset_by * (used - fixed)) % max(1, count - fixed)
        return jnp.zeros((count,), jnp.int32).at[order[jnp.where(places < fixed, places, moved)]].set(jnp.asarray(sizes, jnp.int32))

    sizes = jnp.where(number % 4 == 0, named(crowded, number // 4), named(usual, number - number // 4 - 1))
    mixed = jax.random.permutation(jax.random.fold_in(own, 3), count)
    source_of, sink = mixed[0:count // 2 * 2:2], mixed[1:count // 2 * 2:2]
    margin = jnp.minimum(sizes[source_of] - 1, reach - sizes[sink]) // 2
    margin = jnp.where((source_of == order[0]) | (sink == order[0]) | (sizes[sink] == 0), 0, jnp.maximum(margin, 0))
    moved = jax.random.randint(jax.random.fold_in(own, 4), (count // 2,), 0, 1 << 20) % (margin + 1)
    sizes = sizes.at[source_of].add(-moved).at[sink].add(moved)
    members = jnp.searchsorted(jnp.cumsum(sizes), jnp.arange(rows * top), side="right").astype(jnp.int32)
    grid = members.reshape(top, rows).T
    grid = grid[jax.random.permutation(jax.random.fold_in(own, 1), rows)]
    offset_by = jax.random.randint(jax.random.fold_in(own, 2), (rows, 1), 0, top)
    return jnp.take_along_axis(grid, (jnp.arange(top)[None, :] + offset_by) % top, axis=1)


def load_shares(number_of, total, reach, skew, full):
    weights = [(1 << 20) // math.isqrt(grade ** skew) + 1 for grade in range(1, number_of + 1)]
    largest = reach if full else min(reach, max(-(-total // number_of), total * weights[0] // sum(weights)))
    least = 1 if total - largest >= number_of - 1 else 0
    counts, spare = [largest] + [least] * (number_of - 1), total - largest - least * (number_of - 1)
    while spare > 0:
        free = [i for i in range(1, number_of) if counts[i] < largest] or [i for i in range(1, number_of) if counts[i] < reach]
        pool, budget = sum([weights[i] for i in free]), spare
        for i in free:
            extra = min(reach - counts[i], max(1, budget * weights[i] // pool), spare)
            counts[i] = counts[i] + extra
            spare = spare - extra
    return np.array(counts)


def noise(own_key, dims, scale, bound, shards=(), kind=jnp.bfloat16):
    values = jax.random.normal(own_key, dims, jnp.float32) * scale
    if len(shards) > 0:
        values = steps_of(own_key, dims, shards, -0.22, 0.18) * values
    return jnp.clip(values, min=-bound, max=bound).astype(kind)


def setup_inputs(seed: int = 0) -> dict:
    streams_of = jax.random.split(jax.random.key(seed), 18)
    hidden_in = noise(streams_of[0], (REQ_TOTAL, D), 0.5, 3.0, ((0, 32),))
    attn_gain = jnp.clip(jnp.exp(jax.random.uniform(streams_of[1], (D,), jnp.float32, math.log(0.5), math.log(2.0))), 0.5, 2.0)
    ffn_gain = jnp.clip(jnp.exp(jax.random.uniform(streams_of[2], (D,), jnp.float32, math.log(0.5), math.log(2.0))), 0.5, 2.0)
    w_query = noise(streams_of[3], (D, QH * HD), D ** -0.5, 0.125, ((1, 4),))
    w_key = noise(streams_of[4], (D, KVH * HD), D ** -0.5, 0.125, ((1, 4),))
    w_value = noise(streams_of[5], (D, KVH * HD), D ** -0.5, 0.125, ((1, 4),))
    q_gain = draw_q_gain(jax.random.fold_in(streams_of[17], 71), 0)
    k_gain = jnp.clip(jnp.exp(jax.random.uniform(streams_of[7], (HD,), jnp.float32, math.log(0.5), math.log(2.0))), 0.5, 2.0)
    key_cache = draw_key_cache(jax.random.fold_in(streams_of[17], 71), 0)
    value_cache = noise(streams_of[9], (REQ_TOTAL, KVH, LMAX, HD), 1.0, 6.0, ((0, 32), (1, 4)))
    w_out = noise(streams_of[10], (QH * HD, D), (QH * HD) ** -0.5, 0.09375, ((0, 4),))
    w_router = noise(streams_of[11], (D, EXPERTS), (16 * D) ** -0.5, 0.03125)
    w_gate = noise(streams_of[12], (EXPERTS, D, FF), D ** -0.5, 0.125, ((0, 32), (2, 4)))
    w_up = noise(streams_of[13], (EXPERTS, D, FF), D ** -0.5, 0.125, ((0, 32), (2, 4)))
    w_down = noise(streams_of[14], (EXPERTS, FF, D), FF ** -0.5, 0.21875, ((0, 32), (1, 4)))
    cache_len = draw_cache_len(jax.random.fold_in(streams_of[17], 71), 0)
    expert_ids_keys = jax.random.split(jax.random.fold_in(streams_of[16], 1), REQ_TOTAL // REQ)
    expert_ids_turns = jax.random.permutation(jax.random.fold_in(streams_of[16], 3), REQ_TOTAL // REQ)
    expert_ids = jax.vmap(lambda own, number: assign_block(jax.random.fold_in(streams_of[16], 2), own, number, REQ, EXPERTS, TOPK, CAP, 2))(expert_ids_keys, expert_ids_turns).reshape((REQ_TOTAL, TOPK))
    return dict(hidden_in=hidden_in, attn_gain=attn_gain, ffn_gain=ffn_gain, w_query=w_query, w_key=w_key, w_value=w_value, q_gain=q_gain, k_gain=k_gain, key_cache=key_cache, value_cache=value_cache, w_out=w_out, w_router=w_router, w_gate=w_gate, w_up=w_up, w_down=w_down, cache_len=cache_len, expert_ids=expert_ids)


rope_base = 1000000.0
norm_eps = 1e-06

def rms_scale(values, gain):
    return values * lax.rsqrt(lax.optimization_barrier(jnp.mean(values * values, axis=-1, keepdims=True)) + norm_eps) * gain

def rotate(values, position):
    half_dim = values.shape[-1] // 2
    steps_half = jnp.arange(half_dim, dtype=jnp.float32)
    frequency = rope_base ** (-2.0 * steps_half / values.shape[-1])
    angle = position.astype(jnp.float32)[:, None] * frequency[None, :]
    cosine = jnp.cos(angle)[:, None, :]
    sine = jnp.sin(angle)[:, None, :]
    first = values[..., :half_dim]
    second = values[..., half_dim:]
    return jnp.concatenate([first * cosine - second * sine, second * cosine + first * sine], axis=-1)

def attend(query, key_new, value_new, key_cache, value_cache, cache_len):
    scale = query.shape[-1] ** (-0.5)
    cached = jnp.einsum('rkgd,rkpd->rkgp', query.astype(jnp.float32), key_cache.astype(jnp.float32)) * scale
    own = jnp.einsum('rkgd,rkd->rkg', query.astype(jnp.float32), key_new.astype(jnp.float32)) * scale
    valid = jnp.arange(key_cache.shape[2], dtype=jnp.int32)[None, :] < cache_len[:, None]
    cached = jnp.where(valid[:, None, None, :], cached, -jnp.inf)
    highest = jnp.maximum(lax.optimization_barrier(jnp.max(cached, axis=-1)), own)
    cached_exp = jnp.exp(cached - highest[..., None])
    own_exp = jnp.exp(own - highest)
    denom = lax.optimization_barrier(jnp.sum(cached_exp, axis=-1)) + own_exp
    probs_cache = (cached_exp / denom[..., None]).astype(jnp.bfloat16)
    probs_own = (own_exp / denom).astype(jnp.bfloat16)
    result = jnp.einsum('rkgp,rkpd->rkgd', probs_cache.astype(jnp.float32), value_cache.astype(jnp.float32))
    result = result + probs_own.astype(jnp.float32)[..., None] * value_new.astype(jnp.float32)[:, :, None, :]
    return result.astype(jnp.bfloat16)

def slot_targets(ids, experts_all, capacity):
    expert_axis = jnp.arange(experts_all, dtype=jnp.int32)
    picked = lax.optimization_barrier(jnp.sum((ids[:, :, None] == expert_axis[None, None, :]).astype(jnp.int32), axis=1))
    before = jnp.cumsum(picked, axis=0) - picked
    slot = jnp.take_along_axis(before, ids, axis=1)
    return ids * capacity + slot

def place_rows(targets, values, slot_count):
    slot_axis = jnp.arange(slot_count, dtype=jnp.int32)
    placing = jnp.any(slot_axis[:, None, None] == targets[None, :, :], axis=2).astype(values.dtype)
    return jnp.dot(placing, values, preferred_element_type=jnp.float32).astype(jnp.bfloat16)

def combine_rows(targets, weights, returned):
    slot_axis = jnp.arange(returned.shape[0], dtype=jnp.int32)
    mixing = lax.optimization_barrier(jnp.sum(jnp.where(targets[:, :, None] == slot_axis[None, None, :], weights[:, :, None], 0.0), axis=1))
    return jnp.dot(mixing, returned.astype(jnp.float32), precision=lax.Precision.HIGHEST)

def expert_apply(packed):
    rows_in, gate_w, up_w, down_w = packed
    gate = jnp.dot(rows_in, gate_w, preferred_element_type=jnp.float32)
    upper = jnp.dot(rows_in, up_w, preferred_element_type=jnp.float32)
    active = (jax.nn.silu(gate) * upper).astype(jnp.bfloat16)
    return jnp.dot(active, down_w, preferred_element_type=jnp.float32).astype(jnp.bfloat16)

def reference(hidden_in, attn_gain, ffn_gain, w_query, w_key, w_value, q_gain, k_gain, key_cache, value_cache, w_out, w_router, w_gate, w_up, w_down, cache_len, expert_ids):
    total_rows = hidden_in.shape[0]
    head_dim = q_gain.shape[0]
    kv_heads = key_cache.shape[1]
    residual_in = hidden_in.astype(jnp.float32)
    normed = rms_scale(residual_in, attn_gain).astype(jnp.bfloat16)
    query = jnp.dot(normed, w_query, preferred_element_type=jnp.float32).reshape(total_rows, -1, head_dim)
    key_new = jnp.dot(normed, w_key, preferred_element_type=jnp.float32).reshape(total_rows, kv_heads, head_dim)
    value_new = jnp.dot(normed, w_value, preferred_element_type=jnp.float32).reshape(total_rows, kv_heads, head_dim).astype(jnp.bfloat16)
    query = rotate(rms_scale(query, q_gain), cache_len).astype(jnp.bfloat16).reshape(total_rows, kv_heads, -1, head_dim)
    key_new = rotate(rms_scale(key_new, k_gain), cache_len).astype(jnp.bfloat16)
    attended = attend(query, key_new, value_new, key_cache, value_cache, cache_len).reshape(total_rows, -1)
    mid = residual_in + jnp.dot(attended, w_out, preferred_element_type=jnp.float32)
    ffn_in = rms_scale(mid, ffn_gain).astype(jnp.bfloat16)
    logits = jnp.dot(ffn_in, w_router, preferred_element_type=jnp.float32)
    weights = jax.nn.softmax(jnp.take_along_axis(logits, expert_ids, axis=1), axis=-1)
    group_ids = expert_ids.reshape(N_GRP, REQ, TOPK)
    targets = jax.vmap(slot_targets, in_axes=(0, None, None))(group_ids, EXPERTS, CAP)
    sent = jax.vmap(place_rows, in_axes=(0, 0, None))(targets, ffn_in.reshape(N_GRP, REQ, D), EXPERTS * CAP)
    rows_in = sent.reshape(N_GRP, EXPERTS, CAP, D).transpose(1, 0, 2, 3).reshape(EXPERTS, N_GRP * CAP, D)
    outputs = lax.map(expert_apply, (rows_in, w_gate, w_up, w_down))
    back = outputs.reshape(EXPERTS, N_GRP, CAP, D).transpose(1, 0, 2, 3).reshape(N_GRP, EXPERTS * CAP, D)
    moe = jax.vmap(combine_rows)(targets, weights.reshape(N_GRP, REQ, TOPK), back)
    return (mid + moe.reshape(total_rows, D)).astype(jnp.bfloat16)
```

```python
import jax
import jax.numpy as jnp
from jax import lax
from jax.experimental import pallas as pl
from jax.experimental.pallas import tpu as pltpu
from jax.sharding import PartitionSpec as P

rope_base = 1000000.0
norm_eps = 1e-06
MESH = pl.DeviceIdType.MESH
BF = jnp.bfloat16
F32 = jnp.float32

ORDER_A = ("x", "y", "z")
ORDER_B = ("y", "z", "x")
ORDER_C = ("z", "x", "y")


def rms_scale(values, gain):
    return values * lax.rsqrt(jnp.mean(values * values, axis=-1, keepdims=True) + norm_eps) * gain


def rotate(values, position):
    half_dim = values.shape[-1] // 2
    steps_half = jnp.arange(half_dim, dtype=jnp.float32)
    frequency = rope_base ** (-2.0 * steps_half / values.shape[-1])
    angle = position.astype(jnp.float32)[:, None] * frequency[None, :]
    cosine = jnp.cos(angle)[:, None, :]
    sine = jnp.sin(angle)[:, None, :]
    first = values[..., :half_dim]
    second = values[..., half_dim:]
    return jnp.concatenate(
        [first * cosine - second * sine, second * cosine + first * sine], axis=-1
    )


def attend(query, key_new, value_new, key_cache, value_cache, cache_len):
    scale = query.shape[-1] ** (-0.5)
    cached = (
        jnp.einsum("rkgd,rkpd->rkgp", query, key_cache, preferred_element_type=jnp.float32) * scale
    )
    own = jnp.einsum("rkgd,rkd->rkg", query, key_new, preferred_element_type=jnp.float32) * scale
    valid = jnp.arange(key_cache.shape[2], dtype=jnp.int32)[None, :] < cache_len[:, None]
    cached = jnp.where(valid[:, None, None, :], cached, -jnp.inf)
    highest = jnp.maximum(jnp.max(cached, axis=-1), own)
    cached_exp = jnp.exp(cached - highest[..., None])
    own_exp = jnp.exp(own - highest)
    denom = jnp.sum(cached_exp, axis=-1) + own_exp
    probs_cache = (cached_exp / denom[..., None]).astype(jnp.bfloat16)
    probs_own = (own_exp / denom).astype(jnp.bfloat16)
    result = jnp.einsum(
        "rkgp,rkpd->rkgd", probs_cache, value_cache, preferred_element_type=jnp.float32
    )
    result = (
        result
        + probs_own.astype(jnp.float32)[..., None] * value_new.astype(jnp.float32)[:, :, None, :]
    )
    return result.astype(jnp.bfloat16)


def dot(a, b):
    return jnp.dot(a, b, preferred_element_type=F32)


def coords():
    g = lax.axis_index("grp")
    return {"z": g // 8, "x": (g // 2) % 4, "c": g % 2, "y": lax.axis_index("tp")}


def device(co):
    return ((co["z"] * 4 + co["x"]) * 2 + co["c"], co["y"])


def moved(co, axis, d):
    size = 2 if axis == "c" else 4
    return dict(co, **{axis: (co[axis] + d) % size})


def block(ref, q, free, co):
    at = [slice(None) if a in free else co[a] for a in ("y", "z", "x")]
    return ref.at[q, at[0], at[1], at[2], co["c"]]


def moe_kernel(
    terms, hidden, gain, ids, w_router, wg_hbm, wu_hbm, wd_hbm,
    out_ref,
    wg, wu, wd, tin, ids_all, xa, xs, sel, msel, wslot, oslot, ya, ysib, r1, s1, r2, s2, r3, mid_ref,
    wsem, t_send, t_recv, i_send, i_recv, g_send, g_recv, c_send, c_recv, e_send, e_recv, s_send, s_recv,
):
    co = coords()
    grp = lax.axis_index("grp")
    me_y = co["y"]
    me_c = co["c"]
    sibling = moved(co, "c", 1)

    def remote(src, dst, ss, rs, to):
        return pltpu.make_async_remote_copy(
            src_ref=src, dst_ref=dst, send_sem=ss, recv_sem=rs, device_id=device(to),
            device_id_type=MESH,
        )

    loads = [
        pltpu.make_async_copy(s, d, wsem.at[i])
        for i, (s, d) in enumerate(((wg_hbm, wg), (wu_hbm, wu), (wd_hbm, wd)))
    ]
    for cp in loads:
        cp.start()

    bar = pltpu.get_barrier_semaphore()

    def greet(d, _):
        pl.semaphore_signal(bar, inc=1, device_id=((grp + d) % 32, me_y), device_id_type=MESH)
        return 0

    lax.fori_loop(1, 32, greet, 0)
    for d in (1, 2, 3):
        pl.semaphore_signal(bar, inc=1, device_id=device(moved(co, "y", d)), device_id_type=MESH)
    lane = lax.broadcasted_iota(jnp.int32, (8, 128), 1)
    idv = ids[...]
    ids_all[grp] = jnp.where(lane // 32 == grp % 4, jnp.concatenate([idv] * 4, axis=1), -1)
    pl.semaphore_wait(bar, 34)

    def quarter(v):
        return pl.ds(pl.multiple_of(v * 512, 512), 512)

    t_copies = []
    for d in (1, 2, 3):
        to = moved(co, "y", d)
        cp = remote(terms.at[:, quarter(to["y"])], tin.at[d - 1], t_send.at[d - 1], t_recv.at[d - 1], to)
        cp.start()
        t_copies.append(cp)

    def ids_copy(d):
        return pltpu.make_async_remote_copy(
            src_ref=ids_all.at[grp], dst_ref=ids_all.at[grp], send_sem=i_send.at[d],
            recv_sem=i_recv.at[d], device_id=((grp + d) % 32, me_y), device_id_type=MESH,
        )

    def ids_start(d, _):
        ids_copy(d).start()
        return 0

    lax.fori_loop(1, 32, ids_start, 0)
    mid = hidden[:, quarter(me_y)].astype(F32) + terms[:, quarter(me_y)].astype(F32)
    for d in (1, 2, 3):
        t_copies[d - 1].wait_recv()
        mid = mid + tin[d - 1].astype(F32)
    mid_ref[...] = mid
    sent = (mid * gain[:, quarter(me_y)]).astype(BF)
    for q in range(4):
        xa[q, me_y, co["z"], co["x"], me_c] = sent[:, q * 128 : (q + 1) * 128]

    def ag_copy(q, order, k, d):
        part = block(xa, q, order[:k], co)
        return remote(part, part, g_send.at[q, k, d - 1], g_recv.at[q, k, d - 1], moved(co, order[k], d))

    def sib_copy(q, order, j):
        part = block(xa, q, order[:2], moved(co, order[2], -j))
        return remote(part, part, c_send.at[q, j], c_recv.at[q, j], sibling)

    def each_part(fn):
        fn(0, ORDER_A)
        fn(1, ORDER_B)
        fn(2, ORDER_C)
        pl.when(me_c == 0)(lambda: fn(3, ORDER_A))
        pl.when(me_c == 1)(lambda: fn(3, ORDER_B))

    def ag_start(k):
        def go(q, order):
            if k > 0:
                for d in (1, 2, 3):
                    ag_copy(q, order, k - 1, d).wait_recv()
            for d in (1, 2, 3):
                ag_copy(q, order, k, d).start()
            if k == 2:
                sib_copy(q, order, 0).start()

        each_part(go)

    ag_start(0)

    def ids_wait(d, _):
        ids_copy(d).wait_recv()
        return 0

    lax.fori_loop(1, 32, ids_wait, 0)
    row = lax.broadcasted_iota(jnp.int32, (256, 256), 0)
    col = lax.broadcasted_iota(jnp.int32, (256, 256), 1)
    before = jnp.where((row < col) & (row // 32 == col // 32), 1.0, 0.0).astype(BF)
    lane256 = lax.broadcasted_iota(jnp.int32, (8, 256), 1)
    sub8 = lax.broadcasted_iota(jnp.int32, (8, 256), 0)
    sub32 = lax.broadcasted_iota(jnp.int32, (32, 256), 0)
    sub128 = lax.broadcasted_iota(jnp.int32, (128, 256), 0)

    def make_slots(z):
        halves = []
        for h in (0, 1):
            t = ids_all[z * 8 + h * 4]
            for j in (1, 2, 3):
                t = jnp.maximum(t, ids_all[z * 8 + h * 4 + j])
            halves.append(t)
        idz = jnp.concatenate(halves, axis=1)
        picked = jnp.zeros((8, 256), F32)
        chosen = jnp.zeros((128, 256), F32)
        for k in range(8):
            row_k = idz[k : k + 1, :]
            picked = picked + jnp.where(row_k == grp * 4 + sub8, 1.0, 0.0)
            chosen = chosen + jnp.where(row_k == sub128, 1.0, 0.0)
        rank = dot(picked.astype(BF), before).astype(jnp.int32)
        place = jnp.where(picked > 0.5, (lane256 // 32) * 4 + rank, -1)
        for e in range(4):
            sel[z, e * 32 : (e + 1) * 32, :] = jnp.where(sub32 == place[e : e + 1, :], 1.0, 0.0).astype(BF)
        ms = lax.dot_general(
            sel[z], chosen.astype(BF), (((1,), (1,)), ((), ())), preferred_element_type=F32
        )
        for e in range(4):
            msel[e, z * 32 : (z + 1) * 32, :] = ms[e * 32 : (e + 1) * 32]

    ag_start(1)
    make_slots(0)
    make_slots(1)
    ag_start(2)
    make_slots(2)
    make_slots(3)

    def ag_last(q, order):
        for d in (1, 2, 3):
            ag_copy(q, order, 2, d).wait_recv()
            sib_copy(q, order, d).start()

    each_part(ag_last)

    def ag_sib(q, order):
        for j in range(4):
            sib_copy(q, order, j).wait_recv()

    def select(q):
        for z in range(4):
            for y in range(4):
                rows = dot(sel[z], xa[q, y, z].reshape(256, 128)).astype(BF)
                for e in range(4):
                    xs[e, z * 32 : (z + 1) * 32, y * 512 + q * 128 : y * 512 + (q + 1) * 128] = rows[
                        e * 32 : (e + 1) * 32
                    ]

    ag_sib(0, ORDER_A)
    select(0)
    ag_sib(1, ORDER_B)
    select(1)
    ag_sib(2, ORDER_C)
    select(2)
    pl.when(me_c == 0)(lambda: ag_sib(3, ORDER_A))
    pl.when(me_c == 1)(lambda: ag_sib(3, ORDER_B))
    select(3)

    for cp in loads:
        cp.wait()
    inv_gain = 1.0 / gain[...]
    lane128 = lax.broadcasted_iota(jnp.int32, (128, 128), 1)
    for e in range(4):
        rows = xs[e]
        plain = rows.astype(F32) * inv_gain
        scale = lax.rsqrt(jnp.sum(plain * plain, axis=1, keepdims=True) * (1.0 / 2048) + norm_eps)
        logits = dot(rows, w_router[...]) * scale
        on = msel[e] > 0.5
        top = jnp.max(jnp.where(on, logits, -1e30), axis=1, keepdims=True)
        ex = jnp.where(on, jnp.exp(jnp.where(on, logits - top, 0.0)), 0.0)
        total = jnp.sum(ex, axis=1, keepdims=True)
        mine = jnp.sum(jnp.where(lane128 == grp * 4 + e, ex, 0.0), axis=1, keepdims=True)
        weight = mine / jnp.where(total > 0.0, total, 1.0)
        gate = dot(rows, wg[e]) * scale
        upper = dot(rows, wu[e]) * scale
        active = (gate / (1.0 + jnp.exp(-gate)) * upper).astype(BF)
        res = (dot(active, wd[e]) * weight).astype(BF)
        for z in range(4):
            oslot[z, e * 32 : (e + 1) * 32, :] = res[z * 32 : (z + 1) * 32]

    def pair_copy(z):
        return remote(
            ya.at[:, :, z, :, 1 - me_c], ysib.at[:, :, z], e_send.at[z], e_recv.at[z], sibling
        )

    for z in range(4):
        for y in range(4):
            part = lax.dot_general(
                sel[z], oslot[z, :, y * 512 : (y + 1) * 512], (((0,), (0,)), ((), ())),
                preferred_element_type=F32,
            ).astype(BF)
            for q in range(4):
                ya[q, y, z] = part[:, q * 128 : (q + 1) * 128].reshape(4, 2, 32, 128)
        pair_copy(z).start()
    for z in range(4):
        pair_copy(z).wait()
        for q in range(4):
            mine = ya.at[q, :, z, :, me_c]
            mine[...] = (mine[...].astype(F32) + ysib[q, :, z].astype(F32)).astype(BF)

    def rs_copy(q, order, k, d):
        axis = order[2 - k]
        to = moved(co, axis, d)
        if k == 0:
            src = block(ya, q, [a for a in order if a != axis], to)
            dst = r1.at[q, d - 1]
        elif k == 1:
            left = [a for a in ("y", "z", "x") if a != order[2]]
            src = s1.at[q, to[axis]] if left[0] == axis else s1.at[q, :, to[axis]]
            dst = r2.at[q, d - 1]
        else:
            src = s2.at[q, to[axis]]
            dst = r3.at[q, d - 1]
        return remote(src, dst, s_send.at[q, k, d - 1], s_recv.at[q, k, d - 1], to)

    def rs_start(k):
        def go(q, order):
            for d in (1, 2, 3):
                rs_copy(q, order, k, d).start()

        return go

    def rs_sum(k):
        def go(q, order):
            for d in (1, 2, 3):
                rs_copy(q, order, k, d).wait_recv()
            if k == 0:
                own = block(ya, q, order[:2], co)[...].astype(F32)
                s1[q] = (own + r1[q, 0].astype(F32) + r1[q, 1].astype(F32) + r1[q, 2].astype(F32)).astype(BF)
            elif k == 1:
                axis = order[1]
                left = [a for a in ("y", "z", "x") if a != order[2]]
                own = s1[q, co[axis]] if left[0] == axis else s1[q, :, co[axis]]
                own = own.astype(F32)
                s2[q] = (own + r2[q, 0].astype(F32) + r2[q, 1].astype(F32) + r2[q, 2].astype(F32)).astype(BF)
            else:
                own = s2[q, co[order[0]]].astype(F32)
                cols = slice(q * 128, (q + 1) * 128)
                out_ref[:, cols] = (
                    mid_ref[:, cols]
                    + ((own + r3[q, 0].astype(F32)) + (r3[q, 1].astype(F32) + r3[q, 2].astype(F32)))
                ).astype(BF)

        return go

    each_part(rs_start(0))
    for k in (0, 1):

        def step(q, order, k=k):
            rs_sum(k)(q, order)
            rs_start(k + 1)(q, order)

        each_part(step)
    each_part(rs_sum(2))

    for cp in t_copies:
        cp.wait_send()

    def ids_sent(d, _):
        ids_copy(d).wait_send()
        return 0

    lax.fori_loop(1, 32, ids_sent, 0)

    def sent_all(q, order):
        for k in range(3):
            for d in (1, 2, 3):
                ag_copy(q, order, k, d).wait_send()
                rs_copy(q, order, k, d).wait_send()
        for j in range(4):
            sib_copy(q, order, j).wait_send()

    each_part(sent_all)


def moe(terms, hidden, gain, ids, w_router, w_gate, w_up, w_down):
    vm = pl.BlockSpec(memory_space=pltpu.VMEM)
    hbm = pl.BlockSpec(memory_space=pl.ANY)
    dma = pltpu.SemaphoreType.DMA
    return pl.pallas_call(
        moe_kernel,
        out_shape=jax.ShapeDtypeStruct((32, 512), BF),
        in_specs=[vm] * 5 + [hbm] * 3,
        out_specs=vm,
        scratch_shapes=[
            pltpu.VMEM((4, 2048, 192), BF),
            pltpu.VMEM((4, 2048, 192), BF),
            pltpu.VMEM((4, 192, 2048), BF),
            pltpu.VMEM((3, 32, 512), BF),
            pltpu.VMEM((32, 8, 128), jnp.int32),
            pltpu.VMEM((4, 4, 4, 4, 2, 32, 128), BF),
            pltpu.VMEM((4, 128, 2048), BF),
            pltpu.VMEM((4, 128, 256), BF),
            pltpu.VMEM((4, 128, 128), F32),
            pltpu.VMEM((4, 128, 128), F32),
            pltpu.VMEM((4, 128, 2048), BF),
            pltpu.VMEM((4, 4, 4, 4, 2, 32, 128), BF),
            pltpu.VMEM((4, 4, 4, 4, 32, 128), BF),
            pltpu.VMEM((4, 3, 4, 4, 32, 128), BF),
            pltpu.VMEM((4, 4, 4, 32, 128), BF),
            pltpu.VMEM((4, 3, 4, 32, 128), BF),
            pltpu.VMEM((4, 4, 32, 128), BF),
            pltpu.VMEM((4, 3, 32, 128), BF),
            pltpu.VMEM((32, 512), F32),
            dma((3,)), dma((3,)), dma((3,)), dma((32,)), dma((32,)),
            dma((4, 3, 3)), dma((4, 3, 3)), dma((4, 4)), dma((4, 4)), dma((4,)), dma((4,)),
            dma((4, 3, 3)), dma((4, 3, 3)),
        ],
        compiler_params=pltpu.CompilerParams(
            collective_id=0, has_side_effects=True, vmem_limit_bytes=56 << 20
        ),
        name="moe",
    )(terms, hidden, gain, ids, w_router, w_gate, w_up, w_down)


def per_device(
    hidden_in, attn_gain, ffn_gain, w_query, w_key, w_value, q_gain, k_gain, key_cache,
    value_cache, w_out, w_router, w_gate, w_up, w_down, cache_len, expert_ids,
):
    tok_rows = hidden_in.shape[0]
    head_dim = q_gain.shape[0]
    kv_local = key_cache.shape[1]
    residual_in = hidden_in.astype(jnp.float32)
    normed = rms_scale(residual_in, attn_gain).astype(jnp.bfloat16)
    query = dot(normed, w_query).reshape(tok_rows, -1, head_dim)
    key_new = dot(normed, w_key).reshape(tok_rows, kv_local, head_dim)
    value_new = dot(normed, w_value).reshape(tok_rows, kv_local, head_dim).astype(jnp.bfloat16)
    query = (
        rotate(rms_scale(query, q_gain), cache_len)
        .astype(jnp.bfloat16)
        .reshape(tok_rows, kv_local, -1, head_dim)
    )
    key_new = rotate(rms_scale(key_new, k_gain), cache_len).astype(jnp.bfloat16)
    attended = attend(query, key_new, value_new, key_cache, value_cache, cache_len).reshape(
        tok_rows, -1
    )
    terms = dot(attended, w_out).astype(BF)
    return moe(
        terms, hidden_in, ffn_gain.reshape(1, -1), expert_ids.T, w_router, w_gate, w_up, w_down
    )


def solution(mesh):
    in_specs = (
        P("grp", None), P(), P(), P(None, "tp"), P(None, "tp"), P(None, "tp"), P(), P(),
        P("grp", "tp", None, None), P("grp", "tp", None, None), P("tp", None), P(),
        P("grp", None, "tp"), P("grp", None, "tp"), P("grp", "tp", None), P("grp"), P("grp", None),
    )
    return jax.shard_map(
        per_device, mesh=mesh, in_specs=in_specs, out_specs=P("grp", "tp"), check_vma=False
    )
```

```python
import math

import jax
import jax.numpy as jnp
from jax import lax
from jax.experimental import pallas as pl
from jax.experimental.pallas import tpu as pltpu
from jax.sharding import PartitionSpec as P

rope_base = 1000000.0
norm_eps = 1e-06
MESH = pl.DeviceIdType.MESH
BF = jnp.bfloat16
F32 = jnp.float32

ORDER_A = ("x", "y", "z")
ORDER_B = ("y", "z", "x")
ORDER_C = ("z", "x", "y")


def dot(a, b):
    return jnp.dot(a, b, preferred_element_type=F32)


def dot_t(a, b):
    return lax.dot_general(a, b, (((1,), (1,)), ((), ())), preferred_element_type=F32)


def rms_scale(values, gain):
    return values * lax.rsqrt(jnp.mean(values * values, axis=-1, keepdims=True) + norm_eps) * gain


def coords():
    g = lax.axis_index("grp")
    return {"z": g // 8, "x": (g // 2) % 4, "c": g % 2, "y": lax.axis_index("tp")}


def device(co):
    return ((co["z"] * 4 + co["x"]) * 2 + co["c"], co["y"])


def moved(co, axis, d):
    size = 2 if axis == "c" else 4
    return dict(co, **{axis: (co[axis] + d + size) % size})


def block(ref, q, free, co, half=None):
    at = [slice(None) if a in free else co[a] for a in ("y", "z", "x")]
    if half is not None:
        first = [a in free for a in ("y", "z", "x")].index(True)
        at[first] = slice(2 * half, 2 * half + 2)
    return ref.at[q, co["c"], at[0], at[1], at[2]]


def quarter(v):
    return pl.ds(pl.multiple_of(v * 512, 512), 512)


def strips(ref, at, q):
    return jnp.concatenate([ref[(*at, slice(y * 512 + q * 128, y * 512 + q * 128 + 128))] for y in range(4)], axis=-1)


def layer_kernel(
    hidden_h, again_h, fgain_h, wq_h, wk_h, wv_h, qgain_h, kgain_h, kc_h, vc_h, wo_h, router_h,
    wg_h, wu_h, wd_h, len_h, ids_h,
    out_ref,
    hidden, again, fgain, wq, wk, wv, qgain, kgain, kc, vc, wo, router, wgu, wd, lens, ids,
    qs, att, kn, vn, terms, tin, ids_all, xa, sel, sel_t, msel, gu_acc, lg_acc, ya, ysib,
    r1u, r1, s1, r2, s2, r3, mid_ref,
    in_sem, kv_sem, wo_sem, ex_sem,
    t_send, t_recv, i_send, i_recv, g_send, g_recv, c_send, c_recv, e_send, e_recv, s_send, s_recv,
):
    co = coords()
    grp = lax.axis_index("grp")
    me_y = co["y"]
    me_c = co["c"]
    sibling = moved(co, "c", 1)

    def local(src, dst, sem):
        return pltpu.make_async_copy(src, dst, sem)

    def remote(src, dst, ss, rs, to):
        return pltpu.make_async_remote_copy(
            src_ref=src, dst_ref=dst, send_sem=ss, recv_sem=rs, device_id=device(to),
            device_id_type=MESH,
        )

    small = [
        local(s, d, in_sem.at[i])
        for i, (s, d) in enumerate(
            (
                (hidden_h, hidden), (again_h, again), (len_h, lens), (qgain_h, qgain),
                (kgain_h, kgain), (fgain_h, fgain), (ids_h, ids), (wk_h, wk), (wv_h, wv),
            )
        )
    ]
    wq_copies = [
        local(wq_h.at[:, i * 256 : (i + 1) * 256], wq.at[:, i * 256 : (i + 1) * 256], in_sem.at[9 + i])
        for i in range(4)
    ]

    def kv_copies(i):
        rows = pl.ds(i * 8, 8)
        return (
            local(kc_h.at[rows], kc.at[rows], kv_sem.at[0, i]),
            local(vc_h.at[rows], vc.at[rows], kv_sem.at[1, i]),
        )

    wo_order = (2, 1, 3, 0)

    def wo_copy(d):
        cols = quarter((me_y + d) % 4)
        return local(wo_h.at[:, cols], wo.at[d], wo_sem.at[d])

    expert_copies = [
        local(router_h, router, ex_sem.at[0]),
        local(wg_h, wgu.at[:, 0:192], ex_sem.at[1]),
        local(wu_h, wgu.at[:, 192:384], ex_sem.at[2]),
        local(wd_h, wd, ex_sem.at[3]),
    ]
    for cp in small + wq_copies:
        cp.start()
    for i in range(4):
        for cp in kv_copies(i):
            cp.start()
    for d in wo_order:
        wo_copy(d).start()

    bar = pltpu.get_barrier_semaphore()

    def greet(d, _):
        pl.semaphore_signal(bar, inc=1, device_id=((grp + d) % 32, me_y), device_id_type=MESH)
        return 0

    lax.fori_loop(1, 32, greet, 0)
    for d in (1, 2, 3):
        pl.semaphore_signal(bar, inc=1, device_id=device(moved(co, "y", d)), device_id_type=MESH)

    for cp in small[:7]:
        cp.wait()
    normed = rms_scale(hidden[...].astype(F32), again[...]).astype(BF)
    row32 = lax.broadcasted_iota(jnp.int32, (32, 128), 0)
    lane = lax.broadcasted_iota(jnp.int32, (32, 128), 1)
    position = jnp.zeros((32, 128), jnp.int32)
    for r in range(32):
        position = jnp.where(row32 == r, lens[r], position)
    steps_half = (lane % 64).astype(F32)
    angle = position.astype(F32) * jnp.exp(steps_half * (-2.0 / 128 * math.log(rope_base)))
    cosine = jnp.cos(angle)
    sine = jnp.sin(angle) * jnp.where(lane < 64, -1.0, 1.0)

    def rotate(values):
        return values * cosine + pltpu.roll(values, 64, 1) * sine

    small[7].wait()
    kn[...] = rotate(rms_scale(dot(normed, wk[...]), kgain[...])).astype(BF).astype(F32)
    small[8].wait()
    vn[...] = dot(normed, wv[...]).astype(BF).astype(F32)
    for i in range(4):
        wq_copies[i].wait()
        pair = dot(normed, wq[:, i * 256 : (i + 1) * 256])
        for j in (0, 1):
            qs[:, 2 * i + j, :] = rotate(rms_scale(pair[:, j * 128 : (j + 1) * 128], qgain[...]))

    lane8 = lax.broadcasted_iota(jnp.int32, (8, 128), 1)
    idv = ids[...]
    ids_all[grp] = jnp.where(lane8 // 32 == co["x"], jnp.concatenate([idv] * 4, axis=1), -1)
    pl.semaphore_wait(bar, 34)

    def ids_copy(d):
        return pltpu.make_async_remote_copy(
            src_ref=ids_all.at[grp], dst_ref=ids_all.at[grp], send_sem=i_send.at[d],
            recv_sem=i_recv.at[d], device_id=((grp + d) % 32, me_y), device_id_type=MESH,
        )

    def ids_start(d, _):
        ids_copy(d).start()
        return 0

    lax.fori_loop(1, 32, ids_start, 0)

    lane512 = lax.broadcasted_iota(jnp.int32, (8, 512), 1)
    scale = 128 ** -0.5

    def attend(i, _):
        for cp in kv_copies(i):
            cp.wait()
        scores, owns = [], []
        for j in range(8):
            r = i * 8 + j
            q = qs[r].astype(BF)
            s = dot_t(q, kc[r]) * scale
            scores.append(jnp.where(lane512 < lens[r], s, -jnp.inf))
            owns.append(jnp.sum(q.astype(F32) * kn[pl.ds(r, 1), :], axis=1, keepdims=True) * scale)
        s = jnp.concatenate(scores, axis=0)
        own = jnp.concatenate(owns, axis=0)
        top = jnp.maximum(jnp.max(s, axis=1, keepdims=True), own)
        ex = jnp.exp(s - top)
        ex_own = jnp.exp(own - top)
        denom = jnp.sum(ex, axis=1, keepdims=True) + ex_own
        probs = (ex / denom).astype(BF)
        probs_own = (ex_own / denom).astype(BF).astype(F32)
        for j in range(8):
            r = i * 8 + j
            rows = slice(j * 8, (j + 1) * 8)
            att[r] = dot(probs[rows], vc[r]) + probs_own[rows] * vn[pl.ds(r, 1), :]
        return 0

    lax.fori_loop(0, 4, attend, 0)
    for cp in expert_copies:
        cp.start()

    heads = jnp.concatenate([att[:, h, :].astype(BF) for h in range(8)], axis=1)

    def t_copy(d):
        return remote(terms.at[d - 1], tin.at[d - 1], t_send.at[d - 1], t_recv.at[d - 1], moved(co, "y", d))

    for d in wo_order[:3]:
        wo_copy(d).wait()
        terms[d - 1] = dot(heads, wo[d]).astype(BF)
        t_copy(d).start()
    wo_copy(0).wait()
    mid = hidden[:, quarter(me_y)].astype(F32) + dot(heads, wo[0]).astype(BF).astype(F32)
    for d in (1, 3, 2):
        t_copy(d).wait_recv()
        mid = mid + tin[d - 1].astype(F32)
    mid_ref[...] = mid
    sent = (mid * fgain[:, quarter(me_y)]).astype(BF)
    for q in range(4):
        xa[q, me_c, me_y, co["z"], co["x"]] = sent[:, q * 128 : (q + 1) * 128]

    def each_part(fn):
        fn(0, ORDER_A)
        fn(1, ORDER_B)
        fn(2, ORDER_C)
        last_part(fn)

    def last_part(fn):
        pl.when(me_c == 0)(lambda: fn(3, ORDER_A))
        pl.when(me_c == 1)(lambda: fn(3, ORDER_B))

    def gather(q, part, sem, to):
        return remote(part, part, g_send.at[q, sem], g_recv.at[q, sem], to)

    def stage1(q, order, d):
        return gather(q, block(xa, q, (), co), d - 1, moved(co, order[0], d))

    def stage2(q, order, d):
        return gather(q, block(xa, q, order[:1], co), 2 + d, moved(co, order[1], d))

    def piece(q, order, j, plane):
        at = moved(moved(co, order[1], -j), order[2], plane)
        return block(xa, q, order[:1], at)

    def stage3(q, order, j, way):
        return gather(q, piece(q, order, j, 0), (6 if way > 0 else 10) + j, moved(co, order[2], way))

    relay_way = {0: 1, 1: -1, 3: 1, 2: -1}
    piece_order = (0, 1, 3, 2)

    def relay(q, order, j):
        way = relay_way[j]
        return gather(q, piece(q, order, j, -way), 14 + j, moved(co, order[2], way))

    def over(q, order, plane):
        part = block(xa, q, order[:2], moved(co, order[2], plane))
        return remote(part, part, c_send.at[q, plane % 4], c_recv.at[q, plane % 4], sibling)

    def begin1(q, order):
        for d in (1, 3, 2):
            stage1(q, order, d).start()

    def begin2(q, order):
        for d in (1, 3, 2):
            stage1(q, order, d).wait_recv()
        for d in (1, 3, 2):
            stage2(q, order, d).start()
        stage3(q, order, 0, 1).start()
        stage3(q, order, 0, -1).start()

    def begin3(q, order):
        for j in piece_order[1:]:
            stage2(q, order, j).wait_recv()
            stage3(q, order, j, 1).start()
            stage3(q, order, j, -1).start()
        over(q, order, 0).start()

    def pass_on(q, order):
        for j in piece_order:
            way = relay_way[j]
            stage3(q, order, j, way).wait_recv()
            relay(q, order, j).start()

    def end_near(q, order):
        for j in piece_order:
            stage3(q, order, j, -relay_way[j]).wait_recv()
        over(q, order, -1).start()
        over(q, order, 1).start()

    def end_far(q, order):
        for j in piece_order:
            relay(q, order, j).wait_recv()
        over(q, order, 2).start()

    def end_over(q, order):
        for plane in (0, -1, 1, 2):
            over(q, order, plane).wait_recv()

    each_part(begin1)

    def ids_wait(d, _):
        ids_copy(d).wait()
        return 0

    lax.fori_loop(1, 32, ids_wait, 0)
    row = lax.broadcasted_iota(jnp.int32, (256, 256), 0)
    col = lax.broadcasted_iota(jnp.int32, (256, 256), 1)
    before = jnp.where((row < col) & (row // 32 == col // 32), 1.0, 0.0).astype(BF)
    lane256 = lax.broadcasted_iota(jnp.int32, (8, 256), 1)
    sub8 = lax.broadcasted_iota(jnp.int32, (8, 256), 0)
    sub32 = lax.broadcasted_iota(jnp.int32, (32, 256), 0)
    sub128 = lax.broadcasted_iota(jnp.int32, (128, 256), 0)

    def make_slots(z):
        halves = []
        for c in (0, 1):
            t = ids_all[z * 8 + c]
            for x in (1, 2, 3):
                t = jnp.maximum(t, ids_all[z * 8 + x * 2 + c])
            halves.append(t)
        idz = jnp.concatenate(halves, axis=1)
        picked = jnp.zeros((8, 256), F32)
        chosen = jnp.zeros((128, 256), F32)
        for k in range(8):
            row_k = idz[k : k + 1, :]
            picked = picked + jnp.where(row_k == grp * 4 + sub8, 1.0, 0.0)
            chosen = chosen + jnp.where(row_k == sub128, 1.0, 0.0)
        rank = dot(picked.astype(BF), before).astype(jnp.int32)
        place = jnp.where(picked > 0.5, (lane256 // 32) * 4 + rank, -1)
        mine = jnp.concatenate(
            [jnp.where(sub32 == place[e : e + 1, :], 1.0, 0.0) for e in range(4)], axis=0
        )
        sel[z] = mine.astype(BF)
        sel_t[z] = mine.T.astype(BF)
        ms = dot_t(mine.astype(BF), chosen.astype(BF))
        for e in range(4):
            msel[e, z * 32 : (z + 1) * 32, :] = ms[e * 32 : (e + 1) * 32]

    make_slots(0)
    each_part(begin2)
    make_slots(1)
    make_slots(2)
    each_part(begin3)
    make_slots(3)
    for cp in expert_copies:
        cp.wait()
    each_part(pass_on)
    each_part(end_near)

    inv_gain = 1.0 / fgain[...]
    squares = [None] * 4

    def products(q, first):
        rows_z = [
            dot(
                sel[z],
                jnp.concatenate(
                    [
                        jnp.concatenate([xa[q, c, y, z].reshape(128, 128) for c in (0, 1)], axis=0)
                        for y in range(4)
                    ],
                    axis=1,
                ),
            )
            for z in range(4)
        ]
        inv = jnp.concatenate(
            [inv_gain[:, y * 512 + q * 128 : y * 512 + q * 128 + 128] for y in range(4)], axis=1
        )
        w_r = jnp.concatenate(
            [router[y * 512 + q * 128 : y * 512 + q * 128 + 128, :] for y in range(4)], axis=0
        )
        for e in range(4):
            rows32 = jnp.concatenate([rows_z[z][e * 32 : (e + 1) * 32] for z in range(4)], axis=0)
            plain = rows32 * inv
            square = jnp.sum(plain * plain, axis=1, keepdims=True)
            rows = rows32.astype(BF)
            gu = dot_t(rows, strips(wgu, (e, slice(None)), q))
            lg = dot(rows, w_r)
            if first:
                squares[e] = square
                gu_acc[e] = gu
                lg_acc[e] = lg
            else:
                squares[e] = squares[e] + square
                gu_acc[e] = gu_acc[e] + gu
                lg_acc[e] = lg_acc[e] + lg

    end_far(0, ORDER_A)
    end_far(1, ORDER_B)
    end_far(2, ORDER_C)
    end_over(0, ORDER_A)
    products(0, True)
    last_part(end_far)
    end_over(1, ORDER_B)
    products(1, False)
    end_over(2, ORDER_C)
    products(2, False)
    last_part(end_over)
    products(3, False)

    lane128 = lax.broadcasted_iota(jnp.int32, (128, 128), 1)
    active, weight = [], []
    for e in range(4):
        norm = lax.rsqrt(squares[e] * (1.0 / 2048) + norm_eps)
        logits = lg_acc[e] * norm
        on = msel[e] > 0.5
        top = jnp.max(jnp.where(on, logits, -1e30), axis=1, keepdims=True)
        ex = jnp.where(on, jnp.exp(jnp.where(on, logits - top, 0.0)), 0.0)
        total = jnp.sum(ex, axis=1, keepdims=True)
        mine = jnp.sum(jnp.where(lane128 == grp * 4 + e, ex, 0.0), axis=1, keepdims=True)
        weight.append(mine / jnp.where(total > 0.0, total, 1.0))
        gate = gu_acc[e, :, 0:192] * norm
        upper = gu_acc[e, :, 192:384] * norm
        active.append((gate / (1.0 + jnp.exp(-gate)) * upper).astype(BF))

    def pair_copy(q):
        return remote(ya.at[q, 1 - me_c], ysib.at[q], e_send.at[q], e_recv.at[q], sibling)

    def token_sums(q):
        res = [(dot(active[e], strips(wd, (e, slice(None)), q)) * weight[e]).astype(BF) for e in range(4)]
        for z in range(4):
            slots = jnp.concatenate([res[e][z * 32 : (z + 1) * 32] for e in range(4)], axis=0)
            part = dot(sel_t[z], slots).astype(BF)
            for c in (0, 1):
                for y in range(4):
                    ya[q, c, y, z] = part[c * 128 : (c + 1) * 128, y * 128 : (y + 1) * 128].reshape(4, 32, 128)
        pair_copy(q).start()

    def scatter(q, src, dst, sem, to):
        return remote(src, dst, s_send.at[q, sem], s_recv.at[q, sem], to)

    def first(q, order, what, way):
        side = 0 if way > 0 else 1
        to = moved(co, order[2], way)
        if what == "far":
            src = block(ya, q, order[:2], moved(co, order[2], 2), side)
            return scatter(q, src, r1u.at[q, side], side, to)
        half = 1 - side if what == "near" else side
        src = block(ya, q, order[:2], to, half)
        return scatter(q, src, r1.at[q, side, 2 * half : 2 * half + 2], (2 if what == "near" else 4) + side, to)

    def left_axes(order):
        return [a for a in ("y", "z", "x") if a != order[2]]

    def second(q, order, d):
        axis = order[1]
        to = moved(co, axis, d)
        src = s1.at[q, to[axis]] if left_axes(order)[0] == axis else s1.at[q, :, to[axis]]
        return scatter(q, src, r2.at[q, d - 1], 5 + d, to)

    def third(q, order, d):
        to = moved(co, order[0], d)
        return scatter(q, s2.at[q, to[order[0]]], r3.at[q, d - 1], 8 + d, to)

    def scatter1(q, order):
        first(q, order, "far", 1).start()
        first(q, order, "far", -1).start()
        first(q, order, "near", 1).start()
        first(q, order, "near", -1).start()

    def pair_add(q):
        pair_copy(q).wait()
        own = ya.at[q, me_c]
        own[...] = (own[...].astype(F32) + ysib[q].astype(F32)).astype(BF)

    def scatter_relay(q, order):
        for way, side in ((1, 0), (-1, 1)):
            first(q, order, "far", way).wait_recv()
            mine = block(ya, q, order[:2], moved(co, order[2], way), side)
            mine[...] = (mine[...].astype(F32) + r1u[q, side].astype(F32)).astype(BF)
            first(q, order, "relayed", way).start()

    def scatter2(q, order):
        for way in (1, -1):
            first(q, order, "near", way).wait_recv()
            first(q, order, "relayed", way).wait_recv()
        own = block(ya, q, order[:2], co)[...].astype(F32)
        s1[q] = (own + r1[q, 0].astype(F32) + r1[q, 1].astype(F32)).astype(BF)
        for d in (1, 3, 2):
            second(q, order, d).start()

    def scatter3(q, order):
        for d in (1, 3, 2):
            second(q, order, d).wait_recv()
        own = s1[q, co[order[1]]] if left_axes(order)[0] == order[1] else s1[q, :, co[order[1]]]
        s2[q] = (
            own.astype(F32) + r2[q, 0].astype(F32) + r2[q, 1].astype(F32) + r2[q, 2].astype(F32)
        ).astype(BF)
        for d in (1, 3, 2):
            third(q, order, d).start()

    def finish(q, order):
        for d in (1, 3, 2):
            third(q, order, d).wait_recv()
        own = s2[q, co[order[0]]].astype(F32)
        cols = slice(q * 128, (q + 1) * 128)
        out_ref[:, cols] = (
            mid_ref[:, cols]
            + ((own + r3[q, 0].astype(F32)) + (r3[q, 1].astype(F32) + r3[q, 2].astype(F32)))
        ).astype(BF)

    token_sums(3)
    token_sums(0)
    pair_add(3)
    last_part(scatter1)
    token_sums(1)
    pair_add(0)
    scatter1(0, ORDER_A)
    token_sums(2)
    pair_add(1)
    scatter1(1, ORDER_B)
    last_part(scatter_relay)
    pair_add(2)
    scatter1(2, ORDER_C)

    def order_of_end(fn):
        last_part(fn)
        fn(0, ORDER_A)
        fn(1, ORDER_B)
        fn(2, ORDER_C)

    scatter_relay(0, ORDER_A)
    scatter_relay(1, ORDER_B)
    scatter_relay(2, ORDER_C)
    order_of_end(scatter2)
    order_of_end(scatter3)
    order_of_end(finish)

    for d in (1, 2, 3):
        t_copy(d).wait_send()

    def sent_all(q, order):
        for d in (1, 2, 3):
            stage1(q, order, d).wait_send()
            stage2(q, order, d).wait_send()
            second(q, order, d).wait_send()
            third(q, order, d).wait_send()
        for j in range(4):
            stage3(q, order, j, 1).wait_send()
            stage3(q, order, j, -1).wait_send()
            relay(q, order, j).wait_send()
        for plane in (0, -1, 1, 2):
            over(q, order, plane).wait_send()
        for way in (1, -1):
            for what in ("far", "near", "relayed"):
                first(q, order, what, way).wait_send()

    each_part(sent_all)


def per_device(
    hidden_in, attn_gain, ffn_gain, w_query, w_key, w_value, q_gain, k_gain, key_cache,
    value_cache, w_out, w_router, w_gate, w_up, w_down, cache_len, expert_ids,
):
    hbm = pl.BlockSpec(memory_space=pl.ANY)
    dma = pltpu.SemaphoreType.DMA
    vmem = pltpu.VMEM
    return pl.pallas_call(
        layer_kernel,
        out_shape=jax.ShapeDtypeStruct((32, 512), BF),
        in_specs=[hbm] * 17,
        out_specs=pl.BlockSpec(memory_space=pltpu.VMEM),
        scratch_shapes=[
            vmem((32, 2048), BF), vmem((1, 2048), F32), vmem((1, 2048), F32), vmem((2048, 1024), BF),
            vmem((2048, 128), BF), vmem((2048, 128), BF), vmem((1, 128), F32), vmem((1, 128), F32),
            vmem((32, 512, 128), BF), vmem((32, 512, 128), BF), vmem((4, 1024, 512), BF),
            vmem((2048, 128), BF), vmem((4, 384, 2048), BF), vmem((4, 192, 2048), BF),
            pltpu.SMEM((32,), jnp.int32), vmem((8, 32), jnp.int32),
            vmem((32, 8, 128), F32), vmem((32, 8, 128), F32), vmem((32, 128), F32), vmem((32, 128), F32),
            vmem((3, 32, 512), BF), vmem((3, 32, 512), BF), vmem((32, 8, 128), jnp.int32),
            vmem((4, 2, 4, 4, 4, 32, 128), BF), vmem((4, 128, 256), BF), vmem((4, 256, 128), BF),
            vmem((4, 128, 128), F32), vmem((4, 128, 384), F32), vmem((4, 128, 128), F32),
            vmem((4, 2, 4, 4, 4, 32, 128), BF), vmem((4, 4, 4, 4, 32, 128), BF),
            vmem((4, 2, 2, 4, 32, 128), BF), vmem((4, 2, 4, 4, 32, 128), BF), vmem((4, 4, 4, 32, 128), BF),
            vmem((4, 3, 4, 32, 128), BF), vmem((4, 4, 32, 128), BF), vmem((4, 3, 32, 128), BF),
            vmem((32, 512), F32),
            dma((13,)), dma((2, 4)), dma((4,)), dma((4,)),
            dma((3,)), dma((3,)), dma((32,)), dma((32,)), dma((4, 18)), dma((4, 18)),
            dma((4, 4)), dma((4, 4)), dma((4,)), dma((4,)), dma((4, 12)), dma((4, 12)),
        ],
        compiler_params=pltpu.CompilerParams(
            collective_id=0, has_side_effects=True, vmem_limit_bytes=58 << 20
        ),
        name="layer",
    )(
        hidden_in, attn_gain.reshape(1, -1), ffn_gain.reshape(1, -1), w_query, w_key, w_value,
        q_gain.reshape(1, -1), k_gain.reshape(1, -1), key_cache.reshape(32, 512, 128),
        value_cache.reshape(32, 512, 128), w_out, w_router, w_gate.swapaxes(1, 2),
        w_up.swapaxes(1, 2), w_down, cache_len, expert_ids.T,
    )


def solution(mesh):
    in_specs = (
        P("grp", None), P(), P(), P(None, "tp"), P(None, "tp"), P(None, "tp"), P(), P(),
        P("grp", "tp", None, None), P("grp", "tp", None, None), P("tp", None), P(),
        P("grp", None, "tp"), P("grp", None, "tp"), P("grp", "tp", None), P("grp"), P("grp", None),
    )
    return jax.shard_map(
        per_device, mesh=mesh, in_specs=in_specs, out_specs=P("grp", "tp"), check_vma=False
    )
```

```python
import math

import jax
import jax.numpy as jnp
from jax import lax
from jax.experimental import pallas as pl
from jax.experimental.pallas import tpu as pltpu
from jax.sharding import PartitionSpec as P

rope_base = 1000000.0
norm_eps = 1e-06
MESH = pl.DeviceIdType.MESH
BF = jnp.bfloat16
F32 = jnp.float32

ORDER_A = ("x", "y", "z")
ORDER_B = ("y", "z", "x")
ORDER_C = ("z", "x", "y")


def dot(a, b):
    return jnp.dot(a, b, preferred_element_type=F32)


def dot_t(a, b):
    return lax.dot_general(a, b, (((1,), (1,)), ((), ())), preferred_element_type=F32)


def rms_scale(values, gain):
    return values * lax.rsqrt(jnp.mean(values * values, axis=-1, keepdims=True) + norm_eps) * gain


def coords():
    g = lax.axis_index("grp")
    return {"z": g // 8, "x": (g // 2) % 4, "c": g % 2, "y": lax.axis_index("tp")}


def device(co):
    return ((co["z"] * 4 + co["x"]) * 2 + co["c"], co["y"])


def moved(co, axis, d):
    size = 2 if axis == "c" else 4
    return dict(co, **{axis: (co[axis] + d + size) % size})


def block(ref, q, free, co, half=None):
    at = [slice(None) if a in free else co[a] for a in ("y", "z", "x")]
    if half is not None:
        first = [a in free for a in ("y", "z", "x")].index(True)
        at[first] = slice(2 * half, 2 * half + 2)
    return ref.at[q, co["c"], at[0], at[1], at[2]]


def quarter(v):
    return pl.ds(pl.multiple_of(v * 512, 512), 512)


def strips(ref, at, q):
    return jnp.concatenate([ref[(*at, slice(y * 512 + q * 128, y * 512 + q * 128 + 128))] for y in range(4)], axis=-1)


def layer_kernel(
    hidden_h, again_h, fgain_h, wq_h, wk_h, wv_h, qgain_h, kgain_h, kc_h, vc_h, wo_h, router_h,
    wg_h, wu_h, wd_h, len_h, ids_h,
    out_ref,
    hidden, again, fgain, wq, wk, wv, qgain, kgain, kc, vc, wo, router, wgu, wd, lens, ids,
    qs, att, kn, vn, terms, tin, ids_all, xa, sel, sel_t, msel, gu_acc, lg_acc, ya, ysib,
    r1u, r1, s1, r2, mid_ref, tally,
    in_sem, kv_sem, wo_sem, ex_sem,
    t_send, t_recv, i_send, i_recv, g_send, g_recv, c_recv, e_send, e_recv, s_send, s_recv,
):
    co = coords()
    grp = lax.axis_index("grp")
    me_y = co["y"]
    me_c = co["c"]
    sibling = moved(co, "c", 1)

    def local(src, dst, sem):
        return pltpu.make_async_copy(src, dst, sem)

    def remote(src, dst, ss, rs, to):
        return pltpu.make_async_remote_copy(
            src_ref=src, dst_ref=dst, send_sem=ss, recv_sem=rs, device_id=device(to),
            device_id_type=MESH,
        )

    small = [
        local(s, d, in_sem.at[i])
        for i, (s, d) in enumerate(
            (
                (len_h, lens), (hidden_h, hidden), (again_h, again), (qgain_h, qgain),
                (kgain_h, kgain), (fgain_h, fgain), (ids_h, ids), (wk_h, wk), (wv_h, wv),
            )
        )
    ]
    wq_copies = [
        local(wq_h.at[:, i * 512 : (i + 1) * 512], wq.at[:, i * 512 : (i + 1) * 512], in_sem.at[9 + i])
        for i in range(2)
    ]

    def kv_copies(i):
        rows = slice(i * 16, (i + 1) * 16)
        return (
            local(kc_h.at[rows], kc.at[rows], kv_sem.at[0, i]),
            local(vc_h.at[rows], vc.at[rows], kv_sem.at[1, i]),
        )

    wo_order = (2, 1, 3, 0)

    def wo_copy(d):
        cols = quarter((me_y + d) % 4)
        return local(wo_h.at[:, cols], wo.at[d], wo_sem.at[d])

    expert_copies = [
        local(router_h, router, ex_sem.at[0]),
        local(wg_h, wgu.at[:, 0:192], ex_sem.at[1]),
        local(wu_h, wgu.at[:, 192:384], ex_sem.at[2]),
        local(wd_h, wd, ex_sem.at[3]),
    ]
    for cp in small + wq_copies:
        cp.start()
    for i in range(2):
        for cp in kv_copies(i):
            cp.start()
    for d in wo_order:
        wo_copy(d).start()

    bar = pltpu.get_barrier_semaphore()

    def greet(d, _):
        pl.semaphore_signal(bar, inc=1, device_id=((grp + d) % 32, me_y), device_id_type=MESH)
        return 0

    lax.fori_loop(1, 32, greet, 0)
    for d in (1, 2, 3):
        pl.semaphore_signal(bar, inc=1, device_id=device(moved(co, "y", d)), device_id_type=MESH)

    small[0].wait()
    row32 = lax.broadcasted_iota(jnp.int32, (32, 128), 0)
    lane = lax.broadcasted_iota(jnp.int32, (32, 128), 1)
    position = jnp.zeros((32, 128), jnp.int32)
    for r in range(32):
        position = jnp.where(row32 == r, lens[r], position)
    steps_half = (lane % 64).astype(F32)
    angle = position.astype(F32) * jnp.exp(steps_half * (-2.0 / 128 * math.log(rope_base)))
    cosine = jnp.cos(angle)
    sine = jnp.sin(angle) * jnp.where(lane < 64, -1.0, 1.0)

    def rotate(values):
        return values * cosine + pltpu.roll(values, 64, 1) * sine

    for cp in small[1:7]:
        cp.wait()
    normed = rms_scale(hidden[...].astype(F32), again[...]).astype(BF)
    small[7].wait()
    small[8].wait()
    keys = dot(normed, wk[...])
    vn[...] = dot(normed, wv[...]).astype(BF).astype(F32)
    wq_copies[0].wait()
    q_low = dot(normed, wq[:, 0:512])
    wq_copies[1].wait()
    q_high = dot(normed, wq[:, 512:1024])
    kn[...] = rotate(rms_scale(keys, kgain[...])).astype(BF).astype(F32)
    for h in range(8):
        head = (q_low if h < 4 else q_high)[:, (h % 4) * 128 : (h % 4 + 1) * 128]
        qs[:, h, :] = rotate(rms_scale(head, qgain[...])).astype(BF).astype(F32)

    lane8 = lax.broadcasted_iota(jnp.int32, (8, 128), 1)
    idv = ids[...]
    ids_all[grp] = jnp.where(lane8 // 32 == co["x"], jnp.concatenate([idv] * 4, axis=1), -1)
    pl.semaphore_wait(bar, 34)

    def ids_copy(d):
        return pltpu.make_async_remote_copy(
            src_ref=ids_all.at[grp], dst_ref=ids_all.at[grp], send_sem=i_send,
            recv_sem=i_recv, device_id=((grp + d) % 32, me_y), device_id_type=MESH,
        )

    def ids_start(d, _):
        ids_copy(d).start()
        return 0

    lax.fori_loop(1, 32, ids_start, 0)

    scale = 128 ** -0.5
    lane_request = lax.broadcasted_iota(jnp.int32, (128, 128), 1) // 8
    where_p = lax.broadcasted_iota(jnp.int32, (512, 128), 0)

    def spread(ref, i):
        rows = ref[i * 16 : (i + 1) * 16]
        return jnp.broadcast_to(rows[:, None, :], (16, 8, 128)).reshape(128, 128)

    for i in range(2):
        q = qs[i * 16 : (i + 1) * 16].reshape(128, 128)
        q_t = q.T
        own = jnp.sum((q * spread(kn, i)).T, axis=0, keepdims=True) * scale
        weights = jnp.concatenate(
            [jnp.where(lane_request == j, q_t, 0.0).astype(BF) for j in range(16)], axis=0
        )
        length = jnp.zeros((1, 128), jnp.int32)
        for j in range(16):
            length = jnp.where(lane_request[0:1] == j, lens[i * 16 + j], length)
        kv_copies(i)[0].wait()
        keys_all = jnp.concatenate([kc[i * 16 + j] for j in range(16)], axis=1)
        s = dot(keys_all, weights) * scale
        s = jnp.where(where_p < length, s, -jnp.inf)
        top = jnp.maximum(jnp.max(s, axis=0, keepdims=True), own)
        ex = jnp.exp(s - top)
        ex_own = jnp.exp(own - top)
        denom = jnp.sum(ex, axis=0, keepdims=True) + ex_own
        probs = (ex / denom).T
        probs_own = (ex_own / denom).astype(BF).astype(F32)
        own_terms = jnp.broadcast_to(probs_own, (128, 128)).T * spread(vn, i)
        kv_copies(i)[1].wait()
        rows = [dot(probs[j * 8 : (j + 1) * 8].astype(BF), vc[i * 16 + j]) for j in range(16)]
        att[i * 16 : (i + 1) * 16] = (jnp.concatenate(rows, axis=0) + own_terms).reshape(16, 8, 128)

    for cp in expert_copies:
        cp.start()

    heads = jnp.concatenate([att[:, h, :].astype(BF) for h in range(8)], axis=1)

    def t_copy(d):
        return remote(terms.at[d - 1], tin.at[d - 1], t_send, t_recv.at[d - 1], moved(co, "y", d))

    for d in wo_order[:3]:
        wo_copy(d).wait()
        terms[d - 1] = dot(heads, wo[d]).astype(BF)
        t_copy(d).start()
    wo_copy(0).wait()
    mid = hidden[:, quarter(me_y)].astype(F32) + dot(heads, wo[0]).astype(BF).astype(F32)
    for d in (1, 3, 2):
        t_copy(d).wait_recv()
        mid = mid + tin[d - 1].astype(F32)
    mid_ref[...] = mid
    sent = (mid * fgain[:, quarter(me_y)]).astype(BF)
    for q in range(4):
        xa[q, me_c, me_y, co["z"], co["x"]] = sent[:, q * 128 : (q + 1) * 128]

    def each_part(fn):
        fn(0, ORDER_A)
        fn(1, ORDER_B)
        fn(2, ORDER_C)
        last_part(fn)

    def last_part(fn):
        pl.when(me_c == 0)(lambda: fn(3, ORDER_A))
        pl.when(me_c == 1)(lambda: fn(3, ORDER_B))

    def chunks(n):
        return tally.at[0:n]

    def await_chunks(n, sem):
        pltpu.make_async_copy(chunks(n), chunks(n), sem).wait()

    def gather(q, part, sem, to):
        return remote(part, part, g_send.at[q], g_recv.at[q, sem], to)

    def in_plane(q, order, i, j):
        to = moved(moved(co, order[0], i), order[1], j)
        return gather(q, block(xa, q, (), co), j, to)

    def piece(q, order, j, plane):
        at = moved(moved(co, order[1], -j), order[2], plane)
        return block(xa, q, order[:1], at)

    relay_way = {0: 1, 1: -1, 3: 1, 2: -1}
    piece_order = (0, 1, 3, 2)

    def along(q, order, j, way):
        sem = 4 + j if way == relay_way[j] else 8
        return gather(q, piece(q, order, j, 0), sem, moved(co, order[2], way))

    def relay(q, order, j):
        way = relay_way[j]
        return gather(q, piece(q, order, j, -way), 9, moved(co, order[2], way))

    def over(q, order, plane):
        part = block(xa, q, order[:2], moved(co, order[2], plane))
        return remote(part, part, g_send.at[q], c_recv.at[q], sibling)

    def begin(q, order):
        for j in (2, 1, 3, 0):
            for i in (2, 1, 3, 0):
                if i or j:
                    in_plane(q, order, i, j).start()

    def begin_axis(q, order):
        for j in piece_order:
            await_chunks(4 if j else 3, g_recv.at[q, j])
            along(q, order, j, 1).start()
            along(q, order, j, -1).start()
        over(q, order, 0).start()

    def pass_on(q, order):
        for j in piece_order:
            along(q, order, j, relay_way[j]).wait_recv()
            relay(q, order, j).start()

    def end_near(q, order):
        await_chunks(16, g_recv.at[q, 8])
        over(q, order, -1).start()
        over(q, order, 1).start()

    def end_far(q, order):
        await_chunks(16, g_recv.at[q, 9])
        over(q, order, 2).start()

    def end_over(q, order):
        await_chunks(64, c_recv.at[q])

    each_part(begin)

    others = ids_all.at[0:31]
    pltpu.make_async_copy(others, others, i_recv).wait()
    pltpu.make_async_copy(others, others, i_send).wait()
    row = lax.broadcasted_iota(jnp.int32, (256, 256), 0)
    col = lax.broadcasted_iota(jnp.int32, (256, 256), 1)
    before = jnp.where((row < col) & (row // 32 == col // 32), 1.0, 0.0).astype(BF)
    lane256 = lax.broadcasted_iota(jnp.int32, (8, 256), 1)
    sub8 = lax.broadcasted_iota(jnp.int32, (8, 256), 0)
    sub32 = lax.broadcasted_iota(jnp.int32, (32, 256), 0)
    sub128 = lax.broadcasted_iota(jnp.int32, (128, 256), 0)

    def make_slots(z):
        halves = []
        for c in (0, 1):
            t = ids_all[z * 8 + c]
            for x in (1, 2, 3):
                t = jnp.maximum(t, ids_all[z * 8 + x * 2 + c])
            halves.append(t)
        idz = jnp.concatenate(halves, axis=1)
        picked = jnp.zeros((8, 256), F32)
        chosen = jnp.zeros((128, 256), F32)
        for k in range(8):
            row_k = idz[k : k + 1, :]
            picked = picked + jnp.where(row_k == grp * 4 + sub8, 1.0, 0.0)
            chosen = chosen + jnp.where(row_k == sub128, 1.0, 0.0)
        rank = dot(picked.astype(BF), before).astype(jnp.int32)
        place = jnp.where(picked > 0.5, (lane256 // 32) * 4 + rank, -1)
        mine = jnp.concatenate(
            [jnp.where(sub32 == place[e : e + 1, :], 1.0, 0.0) for e in range(4)], axis=0
        )
        sel[z] = mine.astype(BF)
        sel_t[z] = mine.T.astype(BF)
        ms = dot_t(mine.astype(BF), chosen.astype(BF))
        for e in range(4):
            msel[e, z * 32 : (z + 1) * 32, :] = ms[e * 32 : (e + 1) * 32]

    make_slots(0)
    make_slots(1)
    make_slots(2)
    make_slots(3)
    each_part(begin_axis)
    for cp in expert_copies:
        cp.wait()
    each_part(pass_on)
    each_part(end_near)

    inv_gain = 1.0 / fgain[...]
    squares = [None] * 4

    def products(q, first):
        rows_z = [
            dot(
                sel[z],
                jnp.concatenate(
                    [
                        jnp.concatenate([xa[q, c, y, z].reshape(128, 128) for c in (0, 1)], axis=0)
                        for y in range(4)
                    ],
                    axis=1,
                ),
            )
            for z in range(4)
        ]
        inv = jnp.concatenate(
            [inv_gain[:, y * 512 + q * 128 : y * 512 + q * 128 + 128] for y in range(4)], axis=1
        )
        w_r = jnp.concatenate(
            [router[y * 512 + q * 128 : y * 512 + q * 128 + 128, :] for y in range(4)], axis=0
        )
        for e in range(4):
            rows32 = jnp.concatenate([rows_z[z][e * 32 : (e + 1) * 32] for z in range(4)], axis=0)
            plain = rows32 * inv
            square = jnp.sum(plain * plain, axis=1, keepdims=True)
            rows = rows32.astype(BF)
            gu = dot_t(rows, strips(wgu, (e, slice(None)), q))
            lg = dot(rows, w_r)
            if first:
                squares[e] = square
                gu_acc[e] = gu
                lg_acc[e] = lg
            else:
                squares[e] = squares[e] + square
                gu_acc[e] = gu_acc[e] + gu
                lg_acc[e] = lg_acc[e] + lg

    end_far(0, ORDER_A)
    end_far(1, ORDER_B)
    end_far(2, ORDER_C)
    end_over(0, ORDER_A)
    products(0, True)
    last_part(end_far)
    end_over(1, ORDER_B)
    products(1, False)
    end_over(2, ORDER_C)
    products(2, False)
    last_part(end_over)
    products(3, False)

    lane128 = lax.broadcasted_iota(jnp.int32, (128, 128), 1)
    active, weight = [], []
    for e in range(4):
        norm = lax.rsqrt(squares[e] * (1.0 / 2048) + norm_eps)
        logits = lg_acc[e] * norm
        on = msel[e] > 0.5
        top = jnp.max(jnp.where(on, logits, -1e30), axis=1, keepdims=True)
        ex = jnp.where(on, jnp.exp(jnp.where(on, logits - top, 0.0)), 0.0)
        total = jnp.sum(ex, axis=1, keepdims=True)
        mine = jnp.sum(jnp.where(lane128 == grp * 4 + e, ex, 0.0), axis=1, keepdims=True)
        weight.append(mine / jnp.where(total > 0.0, total, 1.0))
        gate = gu_acc[e, :, 0:192] * norm
        upper = gu_acc[e, :, 192:384] * norm
        active.append((gate / (1.0 + jnp.exp(-gate)) * upper).astype(BF))

    def pair_copy(q):
        return remote(ya.at[q, 1 - me_c], ysib.at[q], e_send, e_recv.at[q], sibling)

    def token_sums(q):
        res = [(dot(active[e], strips(wd, (e, slice(None)), q)) * weight[e]).astype(BF) for e in range(4)]
        for z in range(4):
            slots = jnp.concatenate([res[e][z * 32 : (z + 1) * 32] for e in range(4)], axis=0)
            part = dot(sel_t[z], slots).astype(BF)
            for c in (0, 1):
                for y in range(4):
                    ya[q, c, y, z] = part[c * 128 : (c + 1) * 128, y * 128 : (y + 1) * 128].reshape(4, 32, 128)
        pair_copy(q).start()

    def scatter(q, src, dst, sem, to):
        return remote(src, dst, s_send.at[q], s_recv.at[q, sem], to)

    def first(q, order, what, way):
        side = 0 if way > 0 else 1
        to = moved(co, order[2], way)
        if what == "far":
            src = block(ya, q, order[:2], moved(co, order[2], 2), side)
            return scatter(q, src, r1u.at[q, side], side, to)
        half = 1 - side if what == "near" else side
        src = block(ya, q, order[:2], to, half)
        return scatter(q, src, r1.at[q, side, 2 * half : 2 * half + 2], 2, to)

    def left_axes(order):
        return [a for a in ("y", "z", "x") if a != order[2]]

    def second(q, order, i, j):
        a, b = left_axes(order)
        to = moved(moved(co, a, i), b, j)
        return scatter(q, s1.at[q, to[a], to[b]], r2.at[q, i * 4 + j - 1], 3, to)

    def scatter1(q, order):
        first(q, order, "far", 1).start()
        first(q, order, "far", -1).start()
        first(q, order, "near", 1).start()
        first(q, order, "near", -1).start()

    def pair_add(q):
        pair_copy(q).wait_recv()
        own = ya.at[q, me_c]
        own[...] = (own[...].astype(F32) + ysib[q].astype(F32)).astype(BF)

    def scatter_relay(q, order):
        for way, side in ((1, 0), (-1, 1)):
            first(q, order, "far", way).wait_recv()
            mine = block(ya, q, order[:2], moved(co, order[2], way), side)
            mine[...] = (mine[...].astype(F32) + r1u[q, side].astype(F32)).astype(BF)
            first(q, order, "relayed", way).start()

    def scatter2(q, order):
        pltpu.make_async_copy(r1.at[q], r1.at[q], s_recv.at[q, 2]).wait()
        own = block(ya, q, order[:2], co)[...].astype(F32)
        s1[q] = (own + r1[q, 0].astype(F32) + r1[q, 1].astype(F32)).astype(BF)
        for j in (2, 1, 3, 0):
            for i in (2, 1, 3, 0):
                if i or j:
                    second(q, order, i, j).start()

    def finish(q, order):
        pltpu.make_async_copy(r2.at[q], r2.at[q], s_recv.at[q, 3]).wait()
        a, b = left_axes(order)
        total = s1[q, co[a], co[b]].astype(F32)
        for n in range(15):
            total = total + r2[q, n].astype(F32)
        cols = slice(q * 128, (q + 1) * 128)
        out_ref[:, cols] = (mid_ref[:, cols] + total).astype(BF)

    token_sums(3)
    token_sums(0)
    pair_add(3)
    last_part(scatter1)
    token_sums(1)
    pair_add(0)
    scatter1(0, ORDER_A)
    token_sums(2)
    pair_add(1)
    scatter1(1, ORDER_B)
    last_part(scatter_relay)
    pair_add(2)
    scatter1(2, ORDER_C)

    def order_of_end(fn):
        last_part(fn)
        fn(0, ORDER_A)
        fn(1, ORDER_B)
        fn(2, ORDER_C)

    scatter_relay(0, ORDER_A)
    scatter_relay(1, ORDER_B)
    scatter_relay(2, ORDER_C)
    order_of_end(scatter2)
    order_of_end(finish)

    pltpu.make_async_copy(tin, tin, t_send).wait()

    pltpu.make_async_copy(ysib, ysib, e_send).wait()
    for q in range(4):
        await_chunks(127, g_send.at[q])
        await_chunks(63, s_send.at[q])


def per_device(
    hidden_in, attn_gain, ffn_gain, w_query, w_key, w_value, q_gain, k_gain, key_cache,
    value_cache, w_out, w_router, w_gate, w_up, w_down, cache_len, expert_ids,
):
    hbm = pl.BlockSpec(memory_space=pl.ANY)
    dma = pltpu.SemaphoreType.DMA
    vmem = pltpu.VMEM
    return pl.pallas_call(
        layer_kernel,
        out_shape=jax.ShapeDtypeStruct((32, 512), BF),
        in_specs=[hbm] * 17,
        out_specs=pl.BlockSpec(memory_space=pltpu.VMEM),
        scratch_shapes=[
            vmem((32, 2048), BF), vmem((1, 2048), F32), vmem((1, 2048), F32), vmem((2048, 1024), BF),
            vmem((2048, 128), BF), vmem((2048, 128), BF), vmem((1, 128), F32), vmem((1, 128), F32),
            vmem((32, 512, 128), BF), vmem((32, 512, 128), BF), vmem((4, 1024, 512), BF),
            vmem((2048, 128), BF), vmem((4, 384, 2048), BF), vmem((4, 192, 2048), BF),
            pltpu.SMEM((32,), jnp.int32), vmem((8, 32), jnp.int32),
            vmem((32, 8, 128), F32), vmem((32, 8, 128), F32), vmem((32, 128), F32), vmem((32, 128), F32),
            vmem((3, 32, 512), BF), vmem((3, 32, 512), BF), vmem((32, 8, 128), jnp.int32),
            vmem((4, 2, 4, 4, 4, 32, 128), BF), vmem((4, 128, 256), BF), vmem((4, 256, 128), BF),
            vmem((4, 128, 128), F32), vmem((4, 128, 384), F32), vmem((4, 128, 128), F32),
            vmem((4, 2, 4, 4, 4, 32, 128), BF), vmem((4, 4, 4, 4, 32, 128), BF),
            vmem((4, 2, 2, 4, 32, 128), BF), vmem((4, 2, 4, 4, 32, 128), BF), vmem((4, 4, 4, 32, 128), BF),
            vmem((4, 15, 32, 128), BF),
            vmem((32, 512), F32), vmem((127, 32, 128), BF),
            dma((11,)), dma((2, 2)), dma((4,)), dma((4,)),
            dma, dma((3,)), dma, dma, dma((4,)), dma((4, 10)), dma((4,)), dma, dma((4,)),
            dma((4,)), dma((4, 4)),
        ],
        compiler_params=pltpu.CompilerParams(
            collective_id=0, has_side_effects=True, vmem_limit_bytes=58 << 20
        ),
        name="layer",
    )(
        hidden_in, attn_gain.reshape(1, -1), ffn_gain.reshape(1, -1), w_query, w_key, w_value,
        q_gain.reshape(1, -1), k_gain.reshape(1, -1), key_cache.reshape(32, 512, 128),
        value_cache.reshape(32, 512, 128), w_out, w_router, w_gate.swapaxes(1, 2),
        w_up.swapaxes(1, 2), w_down, cache_len, expert_ids.T,
    )


def solution(mesh):
    in_specs = (
        P("grp", None), P(), P(), P(None, "tp"), P(None, "tp"), P(None, "tp"), P(), P(),
        P("grp", "tp", None, None), P("grp", "tp", None, None), P("tp", None), P(),
        P("grp", None, "tp"), P("grp", None, "tp"), P("grp", "tp", None), P("grp"), P("grp", None),
    )
    return jax.shard_map(
        per_device, mesh=mesh, in_specs=in_specs, out_specs=P("grp", "tp"), check_vma=False
    )
```

```python
import math

import jax
import jax.numpy as jnp
from jax import lax
from jax.experimental import pallas as pl
from jax.experimental.pallas import tpu as pltpu
from jax.sharding import PartitionSpec as P

rope_base = 1000000.0
norm_eps = 1e-06
MESH = pl.DeviceIdType.MESH
BF = jnp.bfloat16
F32 = jnp.float32

ORDER_A = ("x", "y", "z")
ORDER_B = ("y", "z", "x")
ORDER_C = ("z", "x", "y")


def dot(a, b):
    return jnp.dot(a, b, preferred_element_type=F32)


def dot_t(a, b):
    return lax.dot_general(a, b, (((1,), (1,)), ((), ())), preferred_element_type=F32)


def rms_scale(values, gain):
    return values * lax.rsqrt(jnp.mean(values * values, axis=-1, keepdims=True) + norm_eps) * gain


def coords():
    g = lax.axis_index("grp")
    return {"z": g // 8, "x": (g // 2) % 4, "c": g % 2, "y": lax.axis_index("tp")}


def device(co):
    return ((co["z"] * 4 + co["x"]) * 2 + co["c"], co["y"])


def moved(co, axis, d):
    size = 2 if axis == "c" else 4
    return dict(co, **{axis: (co[axis] + d + size) % size})


def block(ref, q, free, co, half=None):
    at = [slice(None) if a in free else co[a] for a in ("y", "z", "x")]
    if half is not None:
        first = [a in free for a in ("y", "z", "x")].index(True)
        at[first] = slice(2 * half, 2 * half + 2)
    return ref.at[q, co["c"], at[0], at[1], at[2]]


def quarter(v):
    return pl.ds(pl.multiple_of(v * 512, 512), 512)


def strips(ref, at, q):
    return jnp.concatenate([ref[(*at, slice(y * 512 + q * 128, y * 512 + q * 128 + 128))] for y in range(4)], axis=-1)


def layer_kernel(
    hidden_h, again_h, fgain_h, wq_h, wk_h, wv_h, qgain_h, kgain_h, kc_h, vc_h, wo_h, router_h,
    wg_h, wu_h, wd_h, len_h, ids_h,
    out_ref,
    hidden, again, fgain, wq, wk, wv, qgain, kgain, kc, vc, wo, router, wgu, wd, lens, ids,
    qs, att, kn, vn, terms, tin, ids_all, xa, sel, sel_t, msel, gu_acc, lg_acc, ya, ysib,
    r1u, r1, s1, r2, mid_ref, tally,
    in_sem, kv_sem, wo_sem, ex_sem,
    t_send, t_recv, i_send, i_recv, g_send, g_recv, c_recv, e_send, e_recv, s_send, s_recv,
):
    co = coords()
    grp = lax.axis_index("grp")
    me_y = co["y"]
    me_c = co["c"]
    sibling = moved(co, "c", 1)

    def local(src, dst, sem):
        return pltpu.make_async_copy(src, dst, sem)

    def remote(src, dst, ss, rs, to):
        return pltpu.make_async_remote_copy(
            src_ref=src, dst_ref=dst, send_sem=ss, recv_sem=rs, device_id=device(to),
            device_id_type=MESH,
        )

    small = [
        local(s, d, in_sem.at[i])
        for i, (s, d) in enumerate(
            (
                (len_h, lens), (hidden_h, hidden), (again_h, again), (qgain_h, qgain),
                (kgain_h, kgain), (fgain_h, fgain), (ids_h, ids), (wk_h, wk), (wv_h, wv),
            )
        )
    ]
    wq_copies = [
        local(wq_h.at[:, i * 512 : (i + 1) * 512], wq.at[:, i * 512 : (i + 1) * 512], in_sem.at[9 + i])
        for i in range(2)
    ]

    def kv_copies(i):
        rows = slice(i * 16, (i + 1) * 16)
        return (
            local(kc_h.at[rows], kc.at[rows], kv_sem.at[0, i]),
            local(vc_h.at[rows], vc.at[rows], kv_sem.at[1, i]),
        )

    wo_order = (2, 1, 3, 0)

    def wo_copy(d):
        cols = quarter((me_y + d) % 4)
        return local(wo_h.at[:, cols], wo.at[d], wo_sem.at[d])

    expert_copies = [
        local(router_h, router, ex_sem.at[0]),
        local(wg_h, wgu.at[:, 0:192], ex_sem.at[1]),
        local(wu_h, wgu.at[:, 192:384], ex_sem.at[2]),
        local(wd_h, wd, ex_sem.at[3]),
    ]
    for cp in small + wq_copies:
        cp.start()
    kv_copies(0)[0].start()

    bar = pltpu.get_barrier_semaphore()

    def greet(d, _):
        pl.semaphore_signal(bar, inc=1, device_id=((grp + d) % 32, me_y), device_id_type=MESH)
        return 0

    lax.fori_loop(1, 32, greet, 0)
    for d in (1, 2, 3):
        pl.semaphore_signal(bar, inc=1, device_id=device(moved(co, "y", d)), device_id_type=MESH)

    small[0].wait()
    row32 = lax.broadcasted_iota(jnp.int32, (32, 128), 0)
    lane = lax.broadcasted_iota(jnp.int32, (32, 128), 1)
    position = jnp.zeros((32, 128), jnp.int32)
    for r in range(32):
        position = jnp.where(row32 == r, lens[r], position)
    steps_half = (lane % 64).astype(F32)
    angle = position.astype(F32) * jnp.exp(steps_half * (-2.0 / 128 * math.log(rope_base)))
    cosine = jnp.cos(angle)
    sine = jnp.sin(angle) * jnp.where(lane < 64, -1.0, 1.0)

    def rotate(values):
        return values * cosine + pltpu.roll(values, 64, 1) * sine

    for cp in small[1:7]:
        cp.wait()
    normed = rms_scale(hidden[...].astype(F32), again[...]).astype(BF)
    small[7].wait()
    small[8].wait()
    keys = dot(normed, wk[...])
    vn[...] = dot(normed, wv[...]).astype(BF).astype(F32)
    wq_copies[0].wait()
    kv_copies(0)[1].start()
    kv_copies(1)[0].start()
    q_low = dot(normed, wq[:, 0:512])
    wq_copies[1].wait()
    kv_copies(1)[1].start()
    for d in wo_order:
        wo_copy(d).start()
    q_high = dot(normed, wq[:, 512:1024])
    kn[...] = rotate(rms_scale(keys, kgain[...])).astype(BF).astype(F32)
    for h in range(8):
        head = (q_low if h < 4 else q_high)[:, (h % 4) * 128 : (h % 4 + 1) * 128]
        qs[:, h, :] = rotate(rms_scale(head, qgain[...])).astype(BF).astype(F32)

    lane8 = lax.broadcasted_iota(jnp.int32, (8, 128), 1)
    idv = ids[...]
    ids_all[grp] = jnp.where(lane8 // 32 == co["x"], jnp.concatenate([idv] * 4, axis=1), -1)
    pl.semaphore_wait(bar, 34)

    def ids_copy(d):
        return pltpu.make_async_remote_copy(
            src_ref=ids_all.at[grp], dst_ref=ids_all.at[grp], send_sem=i_send,
            recv_sem=i_recv, device_id=((grp + d) % 32, me_y), device_id_type=MESH,
        )

    def ids_start(d, _):
        ids_copy(d).start()
        return 0

    lax.fori_loop(1, 32, ids_start, 0)

    scale = 128 ** -0.5
    lane_request = lax.broadcasted_iota(jnp.int32, (128, 128), 1) // 8
    where_p = lax.broadcasted_iota(jnp.int32, (512, 128), 0)

    def spread(ref, i):
        rows = ref[i * 16 : (i + 1) * 16]
        return jnp.broadcast_to(rows[:, None, :], (16, 8, 128)).reshape(128, 128)

    for i in range(2):
        q = qs[i * 16 : (i + 1) * 16].reshape(128, 128)
        own = jnp.sum((q * spread(kn, i)).T, axis=0, keepdims=True) * scale
        length = jnp.zeros((1, 128), jnp.int32)
        for j in range(16):
            length = jnp.where(lane_request[0:1] == j, lens[i * 16 + j], length)
        kv_copies(i)[0].wait()
        s = [dot_t(q[j * 8 : (j + 1) * 8].astype(BF), kc[i * 16 + j]) for j in range(16)]
        s = jnp.concatenate(s, axis=0).T * scale
        s = jnp.where(where_p < length, s, -jnp.inf)
        top = jnp.maximum(jnp.max(s, axis=0, keepdims=True), own)
        ex = jnp.exp(s - top)
        ex_own = jnp.exp(own - top)
        denom = jnp.sum(ex, axis=0, keepdims=True) + ex_own
        probs = (ex / denom).T
        probs_own = (ex_own / denom).astype(BF).astype(F32)
        own_terms = jnp.broadcast_to(probs_own, (128, 128)).T * spread(vn, i)
        kv_copies(i)[1].wait()
        rows = [dot(probs[j * 8 : (j + 1) * 8].astype(BF), vc[i * 16 + j]) for j in range(16)]
        att[i * 16 : (i + 1) * 16] = (jnp.concatenate(rows, axis=0) + own_terms).reshape(16, 8, 128)

    for cp in expert_copies:
        cp.start()

    heads = jnp.concatenate([att[:, h, :].astype(BF) for h in range(8)], axis=1)

    def t_copy(d):
        return remote(terms.at[d - 1], tin.at[d - 1], t_send, t_recv.at[d - 1], moved(co, "y", d))

    for d in wo_order[:3]:
        wo_copy(d).wait()
        terms[d - 1] = dot(heads, wo[d]).astype(BF)
        t_copy(d).start()
    wo_copy(0).wait()
    mid = hidden[:, quarter(me_y)].astype(F32) + dot(heads, wo[0]).astype(BF).astype(F32)
    for d in (1, 3, 2):
        t_copy(d).wait_recv()
        mid = mid + tin[d - 1].astype(F32)
    mid_ref[...] = mid
    sent = (mid * fgain[:, quarter(me_y)]).astype(BF)
    for q in range(4):
        xa[q, me_c, me_y, co["z"], co["x"]] = sent[:, q * 128 : (q + 1) * 128]

    def each_part(fn):
        fn(0, ORDER_A)
        fn(1, ORDER_B)
        fn(2, ORDER_C)
        last_part(fn)

    def last_part(fn):
        pl.when(me_c == 0)(lambda: fn(3, ORDER_A))
        pl.when(me_c == 1)(lambda: fn(3, ORDER_B))

    def chunks(n):
        return tally.at[0:n]

    def await_chunks(n, sem):
        pltpu.make_async_copy(chunks(n), chunks(n), sem).wait()

    def gather(q, part, sem, to):
        return remote(part, part, g_send.at[q], g_recv.at[q, sem], to)

    def in_plane(q, order, i, j):
        to = moved(moved(co, order[0], i), order[1], j)
        return gather(q, block(xa, q, (), co), j, to)

    def piece(q, order, j, plane):
        at = moved(moved(co, order[1], -j), order[2], plane)
        return block(xa, q, order[:1], at)

    relay_way = {0: 1, 1: -1, 3: 1, 2: -1}
    piece_order = (0, 1, 3, 2)

    def along(q, order, j, way):
        sem = 4 + j if way == relay_way[j] else 8
        return gather(q, piece(q, order, j, 0), sem, moved(co, order[2], way))

    def relay(q, order, j):
        way = relay_way[j]
        return gather(q, piece(q, order, j, -way), 9, moved(co, order[2], way))

    def over(q, order, plane):
        part = block(xa, q, order[:2], moved(co, order[2], plane))
        return remote(part, part, g_send.at[q], c_recv.at[q], sibling)

    def begin(q, order):
        for j in (2, 1, 3, 0):
            for i in (2, 1, 3, 0):
                if i or j:
                    in_plane(q, order, i, j).start()

    def begin_axis(q, order):
        for j in piece_order:
            await_chunks(4 if j else 3, g_recv.at[q, j])
            along(q, order, j, 1).start()
            along(q, order, j, -1).start()
        over(q, order, 0).start()

    def pass_on(q, order):
        for j in piece_order:
            along(q, order, j, relay_way[j]).wait_recv()
            relay(q, order, j).start()

    def end_near(q, order):
        await_chunks(16, g_recv.at[q, 8])
        over(q, order, -1).start()
        over(q, order, 1).start()

    def end_far(q, order):
        await_chunks(16, g_recv.at[q, 9])
        over(q, order, 2).start()

    def end_over(q, order):
        await_chunks(64, c_recv.at[q])

    each_part(begin)

    others = ids_all.at[0:31]
    pltpu.make_async_copy(others, others, i_recv).wait()
    pltpu.make_async_copy(others, others, i_send).wait()
    row = lax.broadcasted_iota(jnp.int32, (256, 256), 0)
    col = lax.broadcasted_iota(jnp.int32, (256, 256), 1)
    before = jnp.where((row < col) & (row // 32 == col // 32), 1.0, 0.0).astype(BF)
    lane256 = lax.broadcasted_iota(jnp.int32, (8, 256), 1)
    sub8 = lax.broadcasted_iota(jnp.int32, (8, 256), 0)
    sub32 = lax.broadcasted_iota(jnp.int32, (32, 256), 0)
    sub128 = lax.broadcasted_iota(jnp.int32, (128, 256), 0)

    def make_slots(z):
        halves = []
        for c in (0, 1):
            t = ids_all[z * 8 + c]
            for x in (1, 2, 3):
                t = jnp.maximum(t, ids_all[z * 8 + x * 2 + c])
            halves.append(t)
        idz = jnp.concatenate(halves, axis=1)
        picked = jnp.zeros((8, 256), F32)
        chosen = jnp.zeros((128, 256), F32)
        for k in range(8):
            row_k = idz[k : k + 1, :]
            picked = picked + jnp.where(row_k == grp * 4 + sub8, 1.0, 0.0)
            chosen = chosen + jnp.where(row_k == sub128, 1.0, 0.0)
        rank = dot(picked.astype(BF), before).astype(jnp.int32)
        place = jnp.where(picked > 0.5, (lane256 // 32) * 4 + rank, -1)
        mine = jnp.concatenate(
            [jnp.where(sub32 == place[e : e + 1, :], 1.0, 0.0) for e in range(4)], axis=0
        )
        sel[z] = mine.astype(BF)
        sel_t[z] = mine.T.astype(BF)
        ms = dot_t(mine.astype(BF), chosen.astype(BF))
        for e in range(4):
            msel[e, z * 32 : (z + 1) * 32, :] = ms[e * 32 : (e + 1) * 32]

    make_slots(0)
    make_slots(1)
    make_slots(2)
    make_slots(3)
    each_part(begin_axis)
    for cp in expert_copies:
        cp.wait()
    each_part(pass_on)
    each_part(end_near)

    inv_gain = 1.0 / fgain[...]
    squares = [None] * 4

    def products(q, first):
        rows_z = [
            dot(
                sel[z],
                jnp.concatenate(
                    [
                        jnp.concatenate([xa[q, c, y, z].reshape(128, 128) for c in (0, 1)], axis=0)
                        for y in range(4)
                    ],
                    axis=1,
                ),
            )
            for z in range(4)
        ]
        inv = jnp.concatenate(
            [inv_gain[:, y * 512 + q * 128 : y * 512 + q * 128 + 128] for y in range(4)], axis=1
        )
        w_r = jnp.concatenate(
            [router[y * 512 + q * 128 : y * 512 + q * 128 + 128, :] for y in range(4)], axis=0
        )
        for e in range(4):
            rows32 = jnp.concatenate([rows_z[z][e * 32 : (e + 1) * 32] for z in range(4)], axis=0)
            plain = rows32 * inv
            square = jnp.sum(plain * plain, axis=1, keepdims=True)
            rows = rows32.astype(BF)
            gu = dot_t(rows, strips(wgu, (e, slice(None)), q))
            lg = dot(rows, w_r)
            if first:
                squares[e] = square
                gu_acc[e] = gu
                lg_acc[e] = lg
            else:
                squares[e] = squares[e] + square
                gu_acc[e] = gu_acc[e] + gu
                lg_acc[e] = lg_acc[e] + lg

    end_far(0, ORDER_A)
    end_far(1, ORDER_B)
    end_far(2, ORDER_C)
    end_over(0, ORDER_A)
    products(0, True)
    last_part(end_far)
    end_over(1, ORDER_B)
    products(1, False)
    end_over(2, ORDER_C)
    products(2, False)
    last_part(end_over)
    products(3, False)

    lane128 = lax.broadcasted_iota(jnp.int32, (128, 128), 1)
    active, weight = [], []
    for e in range(4):
        norm = lax.rsqrt(squares[e] * (1.0 / 2048) + norm_eps)
        logits = lg_acc[e] * norm
        on = msel[e] > 0.5
        top = jnp.max(jnp.where(on, logits, -1e30), axis=1, keepdims=True)
        ex = jnp.where(on, jnp.exp(jnp.where(on, logits - top, 0.0)), 0.0)
        total = jnp.sum(ex, axis=1, keepdims=True)
        mine = jnp.sum(jnp.where(lane128 == grp * 4 + e, ex, 0.0), axis=1, keepdims=True)
        weight.append(mine / jnp.where(total > 0.0, total, 1.0))
        gate = gu_acc[e, :, 0:192] * norm
        upper = gu_acc[e, :, 192:384] * norm
        active.append((gate / (1.0 + jnp.exp(-gate)) * upper).astype(BF))

    def pair_copy(q):
        return remote(ya.at[q, 1 - me_c], ysib.at[q], e_send, e_recv.at[q], sibling)

    def token_sums(q):
        res = [(dot(active[e], strips(wd, (e, slice(None)), q)) * weight[e]).astype(BF) for e in range(4)]
        for z in range(4):
            slots = jnp.concatenate([res[e][z * 32 : (z + 1) * 32] for e in range(4)], axis=0)
            part = dot(sel_t[z], slots).astype(BF)
            for c in (0, 1):
                for y in range(4):
                    ya[q, c, y, z] = part[c * 128 : (c + 1) * 128, y * 128 : (y + 1) * 128].reshape(4, 32, 128)
        pair_copy(q).start()

    def scatter(q, src, dst, sem, to):
        return remote(src, dst, s_send.at[q], s_recv.at[q, sem], to)

    def first(q, order, way):
        to = moved(co, order[2], way)
        return scatter(q, block(ya, q, order[:2], to), r1.at[q, way - 1], 0, to)

    def left_axes(order):
        return [a for a in ("y", "z", "x") if a != order[2]]

    def second(q, order, i, j):
        a, b = left_axes(order)
        to = moved(moved(co, a, i), b, j)
        return scatter(q, s1.at[q, to[a], to[b]], r2.at[q, i * 4 + j - 1], 3, to)

    def scatter1(q, order):
        for way in (2, 1, 3):
            first(q, order, way).start()

    def pair_add(q):
        pair_copy(q).wait_recv()
        own = ya.at[q, me_c]
        own[...] = (own[...].astype(F32) + ysib[q].astype(F32)).astype(BF)

    def scatter2(q, order):
        pltpu.make_async_copy(r1.at[q], r1.at[q], s_recv.at[q, 0]).wait()
        own = block(ya, q, order[:2], co)[...].astype(F32)
        s1[q] = (own + r1[q, 0].astype(F32) + r1[q, 1].astype(F32) + r1[q, 2].astype(F32)).astype(BF)
        for j in (2, 1, 3, 0):
            for i in (2, 1, 3, 0):
                if i or j:
                    second(q, order, i, j).start()

    def finish(q, order):
        pltpu.make_async_copy(r2.at[q], r2.at[q], s_recv.at[q, 3]).wait()
        a, b = left_axes(order)
        total = s1[q, co[a], co[b]].astype(F32)
        for n in range(15):
            total = total + r2[q, n].astype(F32)
        cols = slice(q * 128, (q + 1) * 128)
        out_ref[:, cols] = (mid_ref[:, cols] + total).astype(BF)

    token_sums(3)
    token_sums(0)
    pair_add(3)
    last_part(scatter1)
    token_sums(1)
    pair_add(0)
    scatter1(0, ORDER_A)
    token_sums(2)
    pair_add(1)
    scatter1(1, ORDER_B)
    pair_add(2)
    scatter1(2, ORDER_C)

    def order_of_end(fn):
        last_part(fn)
        fn(0, ORDER_A)
        fn(1, ORDER_B)
        fn(2, ORDER_C)

    order_of_end(scatter2)
    order_of_end(finish)

    pltpu.make_async_copy(tin, tin, t_send).wait()

    pltpu.make_async_copy(ysib, ysib, e_send).wait()
    for q in range(4):
        await_chunks(127, g_send.at[q])
        await_chunks(63, s_send.at[q])


def per_device(
    hidden_in, attn_gain, ffn_gain, w_query, w_key, w_value, q_gain, k_gain, key_cache,
    value_cache, w_out, w_router, w_gate, w_up, w_down, cache_len, expert_ids,
):
    hbm = pl.BlockSpec(memory_space=pl.ANY)
    dma = pltpu.SemaphoreType.DMA
    vmem = pltpu.VMEM
    return pl.pallas_call(
        layer_kernel,
        out_shape=jax.ShapeDtypeStruct((32, 512), BF),
        in_specs=[hbm] * 17,
        out_specs=pl.BlockSpec(memory_space=pltpu.VMEM),
        scratch_shapes=[
            vmem((32, 2048), BF), vmem((1, 2048), F32), vmem((1, 2048), F32), vmem((2048, 1024), BF),
            vmem((2048, 128), BF), vmem((2048, 128), BF), vmem((1, 128), F32), vmem((1, 128), F32),
            vmem((32, 512, 128), BF), vmem((32, 512, 128), BF), vmem((4, 1024, 512), BF),
            vmem((2048, 128), BF), vmem((4, 384, 2048), BF), vmem((4, 192, 2048), BF),
            pltpu.SMEM((32,), jnp.int32), vmem((8, 32), jnp.int32),
            vmem((32, 8, 128), F32), vmem((32, 8, 128), F32), vmem((32, 128), F32), vmem((32, 128), F32),
            vmem((3, 32, 512), BF), vmem((3, 32, 512), BF), vmem((32, 8, 128), jnp.int32),
            vmem((4, 2, 4, 4, 4, 32, 128), BF), vmem((4, 128, 256), BF), vmem((4, 256, 128), BF),
            vmem((4, 128, 128), F32), vmem((4, 128, 384), F32), vmem((4, 128, 128), F32),
            vmem((4, 2, 4, 4, 4, 32, 128), BF), vmem((4, 4, 4, 4, 32, 128), BF),
            vmem((4, 2, 2, 4, 32, 128), BF), vmem((4, 3, 4, 4, 32, 128), BF), vmem((4, 4, 4, 32, 128), BF),
            vmem((4, 15, 32, 128), BF),
            vmem((32, 512), F32), vmem((127, 32, 128), BF),
            dma((11,)), dma((2, 2)), dma((4,)), dma((4,)),
            dma, dma((3,)), dma, dma, dma((4,)), dma((4, 10)), dma((4,)), dma, dma((4,)),
            dma((4,)), dma((4, 4)),
        ],
        compiler_params=pltpu.CompilerParams(
            collective_id=0, has_side_effects=True, vmem_limit_bytes=58 << 20
        ),
        name="layer",
    )(
        hidden_in, attn_gain.reshape(1, -1), ffn_gain.reshape(1, -1), w_query, w_key, w_value,
        q_gain.reshape(1, -1), k_gain.reshape(1, -1), key_cache.reshape(32, 512, 128),
        value_cache.reshape(32, 512, 128), w_out, w_router, w_gate.swapaxes(1, 2),
        w_up.swapaxes(1, 2), w_down, cache_len, expert_ids.T,
    )


def solution(mesh):
    in_specs = (
        P("grp", None), P(), P(), P(None, "tp"), P(None, "tp"), P(None, "tp"), P(), P(),
        P("grp", "tp", None, None), P("grp", "tp", None, None), P("tp", None), P(),
        P("grp", None, "tp"), P("grp", None, "tp"), P("grp", "tp", None), P("grp"), P("grp", None),
    )
    return jax.shard_map(
        per_device, mesh=mesh, in_specs=in_specs, out_specs=P("grp", "tp"), check_vma=False
    )
```

```python
import math

import jax
import jax.numpy as jnp
from jax import lax
from jax.experimental import pallas as pl
from jax.experimental.pallas import tpu as pltpu
from jax.sharding import PartitionSpec as P

rope_base = 1000000.0
norm_eps = 1e-06
MESH = pl.DeviceIdType.MESH
BF = jnp.bfloat16
F32 = jnp.float32

ORDER_A = ("x", "y", "z")
ORDER_B = ("y", "z", "x")
ORDER_C = ("z", "x", "y")


def dot(a, b):
    return jnp.dot(a, b, preferred_element_type=F32)


def dot_t(a, b):
    return lax.dot_general(a, b, (((1,), (1,)), ((), ())), preferred_element_type=F32)


def rms_scale(values, gain):
    return values * lax.rsqrt(jnp.mean(values * values, axis=-1, keepdims=True) + norm_eps) * gain


def coords():
    g = lax.axis_index("grp")
    return {"z": g // 8, "x": (g // 2) % 4, "c": g % 2, "y": lax.axis_index("tp")}


def device(co):
    return ((co["z"] * 4 + co["x"]) * 2 + co["c"], co["y"])


def moved(co, axis, d):
    size = 2 if axis == "c" else 4
    return dict(co, **{axis: (co[axis] + d + size) % size})


def block(ref, q, free, co, half=None):
    at = [slice(None) if a in free else co[a] for a in ("y", "z", "x")]
    if half is not None:
        first = [a in free for a in ("y", "z", "x")].index(True)
        at[first] = slice(2 * half, 2 * half + 2)
    return ref.at[q, co["c"], at[0], at[1], at[2]]


def quarter(v):
    return pl.ds(pl.multiple_of(v * 512, 512), 512)


def strips(ref, at, q):
    return jnp.concatenate([ref[(*at, slice(y * 512 + q * 128, y * 512 + q * 128 + 128))] for y in range(4)], axis=-1)


def layer_kernel(
    hidden_h, again_h, fgain_h, wq_h, wk_h, wv_h, qgain_h, kgain_h, kc_h, vc_h, wo_h, router_h,
    wg_h, wu_h, wd_h, len_h, ids_h,
    out_ref,
    hidden, again, fgain, wq, wk, wv, qgain, kgain, kc, vc, wo, router, wgu, wd, lens, ids,
    qs, att, kn, vn, terms, tin, ids_all, xa, sel, sel_t, msel, gu_acc, lg_acc, ya, ysib,
    r1u, r1, s1, r2, mid_ref, tally,
    in_sem, kv_sem, wo_sem, ex_sem,
    t_send, t_recv, i_send, i_recv, g_send, g_recv, c_recv, e_send, e_recv, s_send, s_recv,
):
    co = coords()
    grp = lax.axis_index("grp")
    me_y = co["y"]
    me_c = co["c"]
    sibling = moved(co, "c", 1)

    def local(src, dst, sem):
        return pltpu.make_async_copy(src, dst, sem)

    def remote(src, dst, ss, rs, to):
        return pltpu.make_async_remote_copy(
            src_ref=src, dst_ref=dst, send_sem=ss, recv_sem=rs, device_id=device(to),
            device_id_type=MESH,
        )

    small = [
        local(s, d, in_sem.at[i])
        for i, (s, d) in enumerate(
            (
                (len_h, lens), (hidden_h, hidden), (again_h, again), (qgain_h, qgain),
                (kgain_h, kgain), (fgain_h, fgain), (ids_h, ids), (wk_h, wk), (wv_h, wv),
            )
        )
    ]
    wq_copies = [
        local(wq_h.at[:, i * 512 : (i + 1) * 512], wq.at[:, i * 512 : (i + 1) * 512], in_sem.at[9 + i])
        for i in range(2)
    ]

    def kv_copies(i):
        rows = slice(i * 16, (i + 1) * 16)
        return (
            local(kc_h.at[rows], kc.at[rows], kv_sem.at[0, i]),
            local(vc_h.at[rows], vc.at[rows], kv_sem.at[1, i]),
        )

    wo_order = (2, 1, 3, 0)

    def wo_copy(d):
        cols = quarter((me_y + d) % 4)
        return local(wo_h.at[:, cols], wo.at[d], wo_sem.at[d])

    expert_copies = [
        local(router_h, router, ex_sem.at[0]),
        local(wg_h, wgu.at[:, 0:192], ex_sem.at[1]),
        local(wu_h, wgu.at[:, 192:384], ex_sem.at[2]),
        local(wd_h, wd, ex_sem.at[3]),
    ]
    for cp in small + wq_copies:
        cp.start()
    kv_copies(0)[0].start()

    bar = pltpu.get_barrier_semaphore()

    def greet(d, _):
        pl.semaphore_signal(bar, inc=1, device_id=((grp + d) % 32, me_y), device_id_type=MESH)
        return 0

    lax.fori_loop(1, 32, greet, 0)
    for d in (1, 2, 3):
        pl.semaphore_signal(bar, inc=1, device_id=device(moved(co, "y", d)), device_id_type=MESH)

    small[0].wait()
    row32 = lax.broadcasted_iota(jnp.int32, (32, 128), 0)
    lane = lax.broadcasted_iota(jnp.int32, (32, 128), 1)
    position = jnp.zeros((32, 128), jnp.int32)
    for r in range(32):
        position = jnp.where(row32 == r, lens[r], position)
    steps_half = (lane % 64).astype(F32)
    angle = position.astype(F32) * jnp.exp(steps_half * (-2.0 / 128 * math.log(rope_base)))
    cosine = jnp.cos(angle)
    sine = jnp.sin(angle) * jnp.where(lane < 64, -1.0, 1.0)

    def rotate(values):
        return values * cosine + pltpu.roll(values, 64, 1) * sine

    for cp in small[1:7]:
        cp.wait()
    normed = rms_scale(hidden[...].astype(F32), again[...]).astype(BF)
    small[7].wait()
    small[8].wait()
    keys = dot(normed, wk[...])
    vn[...] = dot(normed, wv[...]).astype(BF).astype(F32)
    wq_copies[0].wait()
    kv_copies(0)[1].start()
    kv_copies(1)[0].start()
    q_low = dot(normed, wq[:, 0:512])
    wq_copies[1].wait()
    kv_copies(1)[1].start()
    for d in wo_order:
        wo_copy(d).start()
    q_high = dot(normed, wq[:, 512:1024])
    kn[...] = rotate(rms_scale(keys, kgain[...])).astype(BF).astype(F32)
    for h in range(8):
        head = (q_low if h < 4 else q_high)[:, (h % 4) * 128 : (h % 4 + 1) * 128]
        qs[:, h, :] = rotate(rms_scale(head, qgain[...])).astype(BF).astype(F32)

    lane8 = lax.broadcasted_iota(jnp.int32, (8, 128), 1)
    idv = ids[...]
    ids_all[grp] = jnp.where(lane8 // 32 == co["x"], jnp.concatenate([idv] * 4, axis=1), -1)

    def ids_copy(d):
        return pltpu.make_async_remote_copy(
            src_ref=ids_all.at[grp], dst_ref=ids_all.at[grp], send_sem=i_send,
            recv_sem=i_recv, device_id=((grp + d) % 32, me_y), device_id_type=MESH,
        )

    def ids_start(d, _):
        ids_copy(d).start()
        return 0


    scale = 128 ** -0.5
    lane_request = lax.broadcasted_iota(jnp.int32, (128, 128), 1) // 8
    where_p = lax.broadcasted_iota(jnp.int32, (512, 128), 0)

    def spread(ref, i):
        rows = ref[i * 16 : (i + 1) * 16]
        return jnp.broadcast_to(rows[:, None, :], (16, 8, 128)).reshape(128, 128)

    for i in range(2):
        q = qs[i * 16 : (i + 1) * 16].reshape(128, 128)
        own = jnp.sum((q * spread(kn, i)).T, axis=0, keepdims=True) * scale
        length = jnp.zeros((1, 128), jnp.int32)
        for j in range(16):
            length = jnp.where(lane_request[0:1] == j, lens[i * 16 + j], length)
        kv_copies(i)[0].wait()
        s = [dot_t(q[j * 8 : (j + 1) * 8].astype(BF), kc[i * 16 + j]) for j in range(16)]
        s = jnp.concatenate(s, axis=0).T * scale
        s = jnp.where(where_p < length, s, -jnp.inf)
        top = jnp.maximum(jnp.max(s, axis=0, keepdims=True), own)
        ex = jnp.exp(s - top)
        ex_own = jnp.exp(own - top)
        denom = jnp.sum(ex, axis=0, keepdims=True) + ex_own
        probs = (ex / denom).T
        probs_own = (ex_own / denom).astype(BF).astype(F32)
        own_terms = jnp.broadcast_to(probs_own, (128, 128)).T * spread(vn, i)
        kv_copies(i)[1].wait()
        rows = [dot(probs[j * 8 : (j + 1) * 8].astype(BF), vc[i * 16 + j]) for j in range(16)]
        att[i * 16 : (i + 1) * 16] = (jnp.concatenate(rows, axis=0) + own_terms).reshape(16, 8, 128)

    for cp in expert_copies:
        cp.start()

    heads = jnp.concatenate([att[:, h, :].astype(BF) for h in range(8)], axis=1)

    def t_copy(d):
        return remote(terms.at[d - 1], tin.at[d - 1], t_send, t_recv.at[d - 1], moved(co, "y", d))

    pl.semaphore_wait(bar, 34)
    for d in wo_order[:3]:
        wo_copy(d).wait()
        terms[d - 1] = dot(heads, wo[d]).astype(BF)
        t_copy(d).start()
    lax.fori_loop(1, 32, ids_start, 0)
    wo_copy(0).wait()
    mid = hidden[:, quarter(me_y)].astype(F32) + dot(heads, wo[0]).astype(BF).astype(F32)
    for d in (1, 3, 2):
        t_copy(d).wait_recv()
        mid = mid + tin[d - 1].astype(F32)
    mid_ref[...] = mid
    sent = (mid * fgain[:, quarter(me_y)]).astype(BF)
    for q in range(4):
        xa[q, me_c, me_y, co["z"], co["x"]] = sent[:, q * 128 : (q + 1) * 128]

    def each_part(fn):
        fn(0, ORDER_A)
        fn(1, ORDER_B)
        fn(2, ORDER_C)
        last_part(fn)

    def last_part(fn):
        pl.when(me_c == 0)(lambda: fn(3, ORDER_A))
        pl.when(me_c == 1)(lambda: fn(3, ORDER_B))

    def chunks(n):
        return tally.at[0:n]

    def await_chunks(n, sem):
        pltpu.make_async_copy(chunks(n), chunks(n), sem).wait()

    def gather(q, part, sem, to):
        return remote(part, part, g_send.at[q], g_recv.at[q, sem], to)

    def in_plane(q, order, i, j):
        to = moved(moved(co, order[0], i), order[1], j)
        return gather(q, block(xa, q, (), co), j, to)

    def piece(q, order, j, plane):
        at = moved(moved(co, order[1], -j), order[2], plane)
        return block(xa, q, order[:1], at)

    relay_way = {0: 1, 1: -1, 3: 1, 2: -1}
    piece_order = (0, 1, 3, 2)

    def along(q, order, j, way):
        sem = 4 + j if way == relay_way[j] else 8
        return gather(q, piece(q, order, j, 0), sem, moved(co, order[2], way))

    def relay(q, order, j):
        way = relay_way[j]
        return gather(q, piece(q, order, j, -way), 9, moved(co, order[2], way))

    def over(q, order, plane):
        part = block(xa, q, order[:2], moved(co, order[2], plane))
        return remote(part, part, g_send.at[q], c_recv.at[q], sibling)

    def begin(q, order):
        for j in (2, 1, 3, 0):
            for i in (2, 1, 3, 0):
                if i or j:
                    in_plane(q, order, i, j).start()

    def begin_axis(q, order):
        for j in piece_order:
            await_chunks(4 if j else 3, g_recv.at[q, j])
            along(q, order, j, 1).start()
            along(q, order, j, -1).start()
        over(q, order, 0).start()

    def pass_on(q, order):
        for j in piece_order:
            along(q, order, j, relay_way[j]).wait_recv()
            relay(q, order, j).start()

    def end_near(q, order):
        await_chunks(16, g_recv.at[q, 8])
        over(q, order, -1).start()
        over(q, order, 1).start()

    def end_far(q, order):
        await_chunks(16, g_recv.at[q, 9])
        over(q, order, 2).start()

    def end_over(q, order):
        await_chunks(64, c_recv.at[q])

    each_part(begin)

    others = ids_all.at[0:31]
    pltpu.make_async_copy(others, others, i_recv).wait()
    pltpu.make_async_copy(others, others, i_send).wait()
    row = lax.broadcasted_iota(jnp.int32, (256, 256), 0)
    col = lax.broadcasted_iota(jnp.int32, (256, 256), 1)
    before = jnp.where((row < col) & (row // 32 == col // 32), 1.0, 0.0).astype(BF)
    lane256 = lax.broadcasted_iota(jnp.int32, (8, 256), 1)
    sub8 = lax.broadcasted_iota(jnp.int32, (8, 256), 0)
    sub32 = lax.broadcasted_iota(jnp.int32, (32, 256), 0)
    sub128 = lax.broadcasted_iota(jnp.int32, (128, 256), 0)

    def make_slots(z):
        halves = []
        for c in (0, 1):
            t = ids_all[z * 8 + c]
            for x in (1, 2, 3):
                t = jnp.maximum(t, ids_all[z * 8 + x * 2 + c])
            halves.append(t)
        idz = jnp.concatenate(halves, axis=1)
        picked = jnp.zeros((8, 256), F32)
        chosen = jnp.zeros((128, 256), F32)
        for k in range(8):
            row_k = idz[k : k + 1, :]
            picked = picked + jnp.where(row_k == grp * 4 + sub8, 1.0, 0.0)
            chosen = chosen + jnp.where(row_k == sub128, 1.0, 0.0)
        rank = dot(picked.astype(BF), before).astype(jnp.int32)
        place = jnp.where(picked > 0.5, (lane256 // 32) * 4 + rank, -1)
        mine = jnp.concatenate(
            [jnp.where(sub32 == place[e : e + 1, :], 1.0, 0.0) for e in range(4)], axis=0
        )
        sel[z] = mine.astype(BF)
        sel_t[z] = mine.T.astype(BF)
        ms = dot_t(mine.astype(BF), chosen.astype(BF))
        for e in range(4):
            msel[e, z * 32 : (z + 1) * 32, :] = ms[e * 32 : (e + 1) * 32]

    make_slots(0)
    make_slots(1)
    make_slots(2)
    make_slots(3)
    each_part(begin_axis)
    for cp in expert_copies:
        cp.wait()
    each_part(pass_on)
    each_part(end_near)

    inv_gain = 1.0 / fgain[...]
    squares = [None] * 4

    def products(q, first):
        rows_z = [
            dot(
                sel[z],
                jnp.concatenate(
                    [
                        jnp.concatenate([xa[q, c, y, z].reshape(128, 128) for c in (0, 1)], axis=0)
                        for y in range(4)
                    ],
                    axis=1,
                ),
            )
            for z in range(4)
        ]
        inv = jnp.concatenate(
            [inv_gain[:, y * 512 + q * 128 : y * 512 + q * 128 + 128] for y in range(4)], axis=1
        )
        w_r = jnp.concatenate(
            [router[y * 512 + q * 128 : y * 512 + q * 128 + 128, :] for y in range(4)], axis=0
        )
        for e in range(4):
            rows32 = jnp.concatenate([rows_z[z][e * 32 : (e + 1) * 32] for z in range(4)], axis=0)
            plain = rows32 * inv
            square = jnp.sum(plain * plain, axis=1, keepdims=True)
            rows = rows32.astype(BF)
            gu = dot_t(rows, strips(wgu, (e, slice(None)), q))
            lg = dot(rows, w_r)
            if first:
                squares[e] = square
                gu_acc[e] = gu
                lg_acc[e] = lg
            else:
                squares[e] = squares[e] + square
                gu_acc[e] = gu_acc[e] + gu
                lg_acc[e] = lg_acc[e] + lg

    end_far(0, ORDER_A)
    end_far(1, ORDER_B)
    end_far(2, ORDER_C)
    end_over(0, ORDER_A)
    products(0, True)
    last_part(end_far)
    end_over(1, ORDER_B)
    products(1, False)
    end_over(2, ORDER_C)
    products(2, False)
    last_part(end_over)
    products(3, False)

    lane128 = lax.broadcasted_iota(jnp.int32, (128, 128), 1)
    active, weight = [], []
    for e in range(4):
        norm = lax.rsqrt(squares[e] * (1.0 / 2048) + norm_eps)
        logits = lg_acc[e] * norm
        on = msel[e] > 0.5
        top = jnp.max(jnp.where(on, logits, -1e30), axis=1, keepdims=True)
        ex = jnp.where(on, jnp.exp(jnp.where(on, logits - top, 0.0)), 0.0)
        total = jnp.sum(ex, axis=1, keepdims=True)
        mine = jnp.sum(jnp.where(lane128 == grp * 4 + e, ex, 0.0), axis=1, keepdims=True)
        weight.append(mine / jnp.where(total > 0.0, total, 1.0))
        gate = gu_acc[e, :, 0:192] * norm
        upper = gu_acc[e, :, 192:384] * norm
        active.append((gate / (1.0 + jnp.exp(-gate)) * upper).astype(BF))

    def pair_copy(q):
        return remote(ya.at[q, 1 - me_c], ysib.at[q], e_send, e_recv.at[q], sibling)

    def token_sums(q):
        res = [(dot(active[e], strips(wd, (e, slice(None)), q)) * weight[e]).astype(BF) for e in range(4)]
        for z in range(4):
            slots = jnp.concatenate([res[e][z * 32 : (z + 1) * 32] for e in range(4)], axis=0)
            part = dot(sel_t[z], slots).astype(BF)
            for c in (0, 1):
                for y in range(4):
                    ya[q, c, y, z] = part[c * 128 : (c + 1) * 128, y * 128 : (y + 1) * 128].reshape(4, 32, 128)
        pair_copy(q).start()

    def scatter(q, src, dst, sem, to):
        return remote(src, dst, s_send.at[q], s_recv.at[q, sem], to)

    def first(q, order, way):
        to = moved(co, order[2], way)
        return scatter(q, block(ya, q, order[:2], to), r1.at[q, way - 1], 0, to)

    def left_axes(order):
        return [a for a in ("y", "z", "x") if a != order[2]]

    def second(q, order, i, j):
        a, b = left_axes(order)
        to = moved(moved(co, a, i), b, j)
        return scatter(q, s1.at[q, to[a], to[b]], r2.at[q, i * 4 + j - 1], 3, to)

    def scatter1(q, order):
        for way in (2, 1, 3):
            first(q, order, way).start()

    def pair_add(q):
        pair_copy(q).wait_recv()
        own = ya.at[q, me_c]
        own[...] = (own[...].astype(F32) + ysib[q].astype(F32)).astype(BF)

    def scatter2(q, order):
        pltpu.make_async_copy(r1.at[q], r1.at[q], s_recv.at[q, 0]).wait()
        own = block(ya, q, order[:2], co)[...].astype(F32)
        s1[q] = (own + r1[q, 0].astype(F32) + r1[q, 1].astype(F32) + r1[q, 2].astype(F32)).astype(BF)
        for j in (2, 1, 3, 0):
            for i in (2, 1, 3, 0):
                if i or j:
                    second(q, order, i, j).start()

    def finish(q, order):
        pltpu.make_async_copy(r2.at[q], r2.at[q], s_recv.at[q, 3]).wait()
        a, b = left_axes(order)
        total = s1[q, co[a], co[b]].astype(F32)
        for n in range(15):
            total = total + r2[q, n].astype(F32)
        cols = slice(q * 128, (q + 1) * 128)
        out_ref[:, cols] = (mid_ref[:, cols] + total).astype(BF)

    token_sums(3)
    token_sums(0)
    pair_add(3)
    last_part(scatter1)
    token_sums(1)
    pair_add(0)
    scatter1(0, ORDER_A)
    token_sums(2)
    pair_add(1)
    scatter1(1, ORDER_B)
    pair_add(2)
    scatter1(2, ORDER_C)

    def order_of_end(fn):
        last_part(fn)
        fn(0, ORDER_A)
        fn(1, ORDER_B)
        fn(2, ORDER_C)

    order_of_end(scatter2)
    order_of_end(finish)

    pltpu.make_async_copy(tin, tin, t_send).wait()

    pltpu.make_async_copy(ysib, ysib, e_send).wait()
    for q in range(4):
        await_chunks(127, g_send.at[q])
        await_chunks(63, s_send.at[q])


def per_device(
    hidden_in, attn_gain, ffn_gain, w_query, w_key, w_value, q_gain, k_gain, key_cache,
    value_cache, w_out, w_router, w_gate, w_up, w_down, cache_len, expert_ids,
):
    hbm = pl.BlockSpec(memory_space=pl.ANY)
    dma = pltpu.SemaphoreType.DMA
    vmem = pltpu.VMEM
    return pl.pallas_call(
        layer_kernel,
        out_shape=jax.ShapeDtypeStruct((32, 512), BF),
        in_specs=[hbm] * 17,
        out_specs=pl.BlockSpec(memory_space=pltpu.VMEM),
        scratch_shapes=[
            vmem((32, 2048), BF), vmem((1, 2048), F32), vmem((1, 2048), F32), vmem((2048, 1024), BF),
            vmem((2048, 128), BF), vmem((2048, 128), BF), vmem((1, 128), F32), vmem((1, 128), F32),
            vmem((32, 512, 128), BF), vmem((32, 512, 128), BF), vmem((4, 1024, 512), BF),
            vmem((2048, 128), BF), vmem((4, 384, 2048), BF), vmem((4, 192, 2048), BF),
            pltpu.SMEM((32,), jnp.int32), vmem((8, 32), jnp.int32),
            vmem((32, 8, 128), F32), vmem((32, 8, 128), F32), vmem((32, 128), F32), vmem((32, 128), F32),
            vmem((3, 32, 512), BF), vmem((3, 32, 512), BF), vmem((32, 8, 128), jnp.int32),
            vmem((4, 2, 4, 4, 4, 32, 128), BF), vmem((4, 128, 256), BF), vmem((4, 256, 128), BF),
            vmem((4, 128, 128), F32), vmem((4, 128, 384), F32), vmem((4, 128, 128), F32),
            vmem((4, 2, 4, 4, 4, 32, 128), BF), vmem((4, 4, 4, 4, 32, 128), BF),
            vmem((4, 2, 2, 4, 32, 128), BF), vmem((4, 3, 4, 4, 32, 128), BF), vmem((4, 4, 4, 32, 128), BF),
            vmem((4, 15, 32, 128), BF),
            vmem((32, 512), F32), vmem((127, 32, 128), BF),
            dma((11,)), dma((2, 2)), dma((4,)), dma((4,)),
            dma, dma((3,)), dma, dma, dma((4,)), dma((4, 10)), dma((4,)), dma, dma((4,)),
            dma((4,)), dma((4, 4)),
        ],
        compiler_params=pltpu.CompilerParams(
            collective_id=0, has_side_effects=True, vmem_limit_bytes=58 << 20
        ),
        name="layer",
    )(
        hidden_in, attn_gain.reshape(1, -1), ffn_gain.reshape(1, -1), w_query, w_key, w_value,
        q_gain.reshape(1, -1), k_gain.reshape(1, -1), key_cache.reshape(32, 512, 128),
        value_cache.reshape(32, 512, 128), w_out, w_router, w_gate.swapaxes(1, 2),
        w_up.swapaxes(1, 2), w_down, cache_len, expert_ids.T,
    )


def solution(mesh):
    in_specs = (
        P("grp", None), P(), P(), P(None, "tp"), P(None, "tp"), P(None, "tp"), P(), P(),
        P("grp", "tp", None, None), P("grp", "tp", None, None), P("tp", None), P(),
        P("grp", None, "tp"), P("grp", None, "tp"), P("grp", "tp", None), P("grp"), P("grp", None),
    )
    return jax.shard_map(
        per_device, mesh=mesh, in_specs=in_specs, out_specs=P("grp", "tp"), check_vma=False
    )
```
